256 devices in a mesh: dp: 4 (over y_hi, core), ctx: 64 (over y_lo, x, z).
Axes of the slice: x: 4, y: 4 (y_hi: 2, y_lo: 2; y = y_hi * 2 + y_lo), z: 8, core: 2. Of those that a mesh axis runs over, the one named last changes fastest.
Arguments:
- inputs: bfloat16 [4, 8192, 512], P('dp', 'ctx'), may hold values from -6 to 6
- grad_out: bfloat16 [4, 8192, 512], P('dp', 'ctx'), may hold values from -6 to 6
- log_dt: float32 [512], replicated, as said below
- log_a_re: float32 [512, 64], replicated, may hold values from -1.5 to 0.5
- a_im: float32 [512, 64], replicated, may hold values from -100 to 100
- c_re: float32 [512, 64], replicated, may hold values from -6 to 6
- c_im: float32 [512, 64], replicated, may hold values from -6 to 6
- skip_gain: float32 [512], replicated, may hold values from -6 to 6
Outputs:
- grad_inputs: bfloat16 [4, 8192, 512], P('dp', 'ctx')
- grad_log_dt: float32 [512], replicated
- grad_log_a_re: float32 [512, 64], replicated
- grad_a_im: float32 [512, 64], replicated
- grad_c_re: float32 [512, 64], replicated
- grad_c_im: float32 [512, 64], replicated
- grad_skip: float32 [512], replicated
The draws below stay inside these ranges and needn't reach their ends.
Inputs may be any that keep to these rules, and one draw needn't show every extreme that they name: exp(log_dt) is positive and below one.
All inputs are finite; a program needn't handle non-finite values.
Results may differ from the reference program's by a relative error of at most 0.013.
Values may be sent and summed in bfloat16 or wider, within the bound.
No kernel may reach another device: no remote copies, remote signals or barrier semaphores. Data moves between devices by JAX's collectives and lax.ppermute only.
A program may use at most 64 MiB of HBM per device.

```python
import math
import jax
import jax.numpy as jnp
from jax import lax

H = 512
N = 64
SEQ = 8192
BATCH = 4
POINTS = 16384


def draw_log_dt(key, part):
    key = jax.random.fold_in(key, 11)
    lower = math.log(0.5)
    upper = math.log(500.0)
    values = jax.random.uniform(key, (H,), jnp.float32, lower, upper)
    return values - jnp.float32(math.log(SEQ))


def shard_levels(rng, shape, cuts, least, high):
    factor_of = 1.0
    for dim, blocks in cuts:
        heights = jax.random.uniform(jax.random.fold_in(jax.random.fold_in(rng, 6), dim), (blocks,), jnp.float32, least / len(cuts), high / len(cuts))
        factor_of = factor_of * jnp.repeat(jnp.exp(heights), shape[dim] // blocks).reshape((-1,) + (1,) * (len(shape) - 1 - dim))
    return factor_of


def centred(stream_key, dims, width, bound, cuts=(), held_as=jnp.bfloat16):
    gain = shard_levels(stream_key, dims, cuts, -0.22, 0.18) if cuts else 1.0
    result = jax.random.normal(stream_key, dims, jnp.float32) * width * gain
    return jnp.minimum(jnp.maximum(result, -bound), bound).astype(held_as)


def setup_inputs(seed: int = 0) -> dict:
    seeds = jax.random.split(jax.random.key(seed), 9)
    inputs = centred(seeds[0], (BATCH, SEQ, H), 1.0, 6.0, ((0, 4), (1, 64)))
    grad_out = centred(seeds[1], (BATCH, SEQ, H), 1.0, 6.0, ((0, 4), (1, 64)))
    log_dt = draw_log_dt(jax.random.fold_in(seeds[8], 71), 0)
    log_a_re = jnp.clip(jax.random.uniform(seeds[3], (H, N), jnp.float32, -1.5, 0.5), -1.5, 0.5)
    a_im = jnp.clip(jax.random.uniform(seeds[4], (H, N), jnp.float32, -100.0, 100.0), -100.0, 100.0)
    c_re = centred(seeds[5], (H, N), 1.0, 6.0, (), jnp.float32)
    c_im = centred(seeds[6], (H, N), 1.0, 6.0, (), jnp.float32)
    skip_gain = centred(seeds[7], (H,), 1.0, 6.0, (), jnp.float32)
    return dict(inputs=inputs, grad_out=grad_out, log_dt=log_dt, log_a_re=log_a_re, a_im=a_im, c_re=c_re, c_im=c_im, skip_gain=skip_gain)


def kernel_block(log_dt, log_a_re, a_im, c_re, c_im, positions):
    step_size = jnp.exp(log_dt)[:, None]
    pole_re = -jnp.exp(log_a_re)
    w_re = step_size * pole_re
    w_im = step_size * a_im
    growth = jnp.exp(w_re)
    half_sin = jnp.sin(0.5 * w_im)
    e_re = jnp.expm1(w_re) * jnp.cos(w_im) - 2.0 * half_sin * half_sin
    e_im = growth * jnp.sin(w_im)
    n_re = e_re * c_re - e_im * c_im
    n_im = e_re * c_im + e_im * c_re
    modulus = pole_re * pole_re + a_im * a_im
    ct_re = (n_re * pole_re + n_im * a_im) / modulus
    ct_im = (n_im * pole_re - n_re * a_im) / modulus
    phase = w_im[:, :, None] * positions
    decays = jnp.exp(w_re[:, :, None] * positions)
    wave_re = decays * jnp.cos(phase)
    wave_im = decays * jnp.sin(phase)
    return 2.0 * lax.optimization_barrier(jnp.sum(ct_re[:, :, None] * wave_re - ct_im[:, :, None] * wave_im, axis=1))

def reference(inputs, grad_out, log_dt, log_a_re, a_im, c_re, c_im, skip_gain):
    chan_block = 16 if H % 16 == 0 else H
    block_count = H // chan_block
    positions = jnp.arange(SEQ, dtype=jnp.float32)

    def split(source):
        return source.reshape((block_count, chan_block) + source.shape[1:])
    input_blocks = jnp.moveaxis(inputs.reshape(BATCH, SEQ, block_count, chan_block), 2, 0)
    output_blocks = jnp.moveaxis(grad_out.reshape(BATCH, SEQ, block_count, chan_block), 2, 0)

    def channel_step(operands):
        first, second, third, fourth, fifth, gain_blk, input_blk, output_blk = operands

        def local_kernel(arg_one, arg_two, arg_three, arg_four, arg_five):
            return kernel_block(arg_one, arg_two, arg_three, arg_four, arg_five, positions)
        kernel, pull = jax.vjp(local_kernel, first, second, third, fourth, fifth)
        input_f = input_blk.astype(jnp.float32)
        output_f = output_blk.astype(jnp.float32)
        input_spec = jnp.fft.fft(input_f, n=POINTS, axis=1)
        output_spec = jnp.fft.fft(output_f, n=POINTS, axis=1)
        kernel_spec = jnp.fft.fft(kernel, n=POINTS, axis=1)
        lag_spec = lax.optimization_barrier(jnp.sum(output_spec * jnp.conj(input_spec), axis=0))
        lag_vals = jnp.fft.ifft(lag_spec, axis=0)[:SEQ].real
        back = jnp.fft.ifft(output_spec * jnp.conj(kernel_spec.T)[None], axis=1)[:, :SEQ].real
        grad_blk = (back + gain_blk * output_f).astype(jnp.bfloat16)
        pulled = pull(lag_vals.T)
        skip_part = lax.optimization_barrier(jnp.sum(output_f * input_f, axis=(0, 1)))
        return (grad_blk, pulled[0], pulled[1], pulled[2], pulled[3], pulled[4], skip_part)
    results = lax.map(channel_step, (split(log_dt), split(log_a_re), split(a_im), split(c_re), split(c_im), split(skip_gain), input_blocks, output_blocks))
    grad_inputs = jnp.moveaxis(results[0], 0, 2).reshape(BATCH, SEQ, H)
    rest = [item.reshape((H,) + item.shape[2:]) for item in results[1:]]
    return (grad_inputs, rest[0], rest[1], rest[2], rest[3], rest[4], rest[5])
```

```python
import functools

import jax
import jax.numpy as jnp
from jax import lax
from jax.experimental import pallas as pl
from jax.experimental.pallas import tpu as pltpu
from jax.sharding import PartitionSpec as P

AXES = ("dp", "ctx")
F32 = jnp.float32
BF16 = jnp.bfloat16
ROWS_IN = 4
ROWS_OUT = 8
FLIP = (((1,), (1,)), ((), ()))
PLAIN = (((1,), (0,)), ((), ()))
OUTER = (((0,), (0,)), ((), ()))


def halves(value):
    high = value.astype(BF16)
    low = (value - high.astype(F32)).astype(BF16)
    return (high, low)


def dot(a, b, dims):
    return lax.dot_general(a, b, dims, preferred_element_type=F32)


def send_kernel(inputs_ref, grad_ref, out_ref, rows):
    owners = rows.shape[0] // ROWS_IN
    for part, ref in enumerate((inputs_ref, grad_ref)):
        block = ref[...].astype(F32)
        for half in range(2):
            piece = block[:, half * owners : (half + 1) * owners].T
            rows[pl.ds(2 * part + half, owners, stride=ROWS_IN), :] = piece
    out_ref[...] = rows[...].astype(BF16)


def table_kernel(cols_ref, fwd_hi, fwd_lo, rev_hi, rev_lo, mix_hi, mix_lo, band_hi, band_lo):
    poles = cols_ref.shape[0]
    half = poles // 2
    span = poles
    w_re, w_im = cols_ref[:, 0:1], cols_ref[:, 1:2]
    ct_re, ct_im = cols_ref[:, 2:3], cols_ref[:, 3:4]
    lane = lax.broadcasted_iota(jnp.int32, (poles, span), 1)
    sub = lax.broadcasted_iota(jnp.int32, (poles, span), 0)
    first = sub < half

    def spread(value):
        return jnp.concatenate([jnp.where(first, value, 0.0), jnp.where(first, 0.0, value)], axis=1)

    def put(hi_ref, lo_ref, part, value):
        hi, lo = halves(spread(value))
        hi_ref[part * poles : (part + 1) * poles, :] = hi
        lo_ref[part * poles : (part + 1) * poles, :] = lo

    step = lane.astype(F32)
    grow = jnp.exp(w_re * step)
    turn = w_im * step
    f_re, f_im = grow * jnp.cos(turn), grow * jnp.sin(turn)
    put(fwd_hi, fwd_lo, 0, f_re)
    put(fwd_hi, fwd_lo, 1, f_im)
    put(fwd_hi, fwd_lo, 2, f_re * step)
    put(fwd_hi, fwd_lo, 3, f_im * step)
    back = (span - lane).astype(F32)
    shrink = jnp.exp(w_re * back)
    twist = w_im * back
    h_re, h_im = shrink * jnp.cos(twist), shrink * jnp.sin(twist)
    put(rev_hi, rev_lo, 0, h_re)
    put(rev_hi, rev_lo, 1, h_im)
    put(rev_hi, rev_lo, 2, h_re * back)
    put(rev_hi, rev_lo, 3, h_im * back)
    put(mix_hi, mix_lo, 0, 2.0 * (ct_re * h_re - ct_im * h_im))
    put(mix_hi, mix_lo, 1, -2.0 * (ct_re * h_im + ct_im * h_re))
    taps = 2.0 * (ct_re * f_re - ct_im * f_im)
    upper = lane >= sub
    zero = jnp.zeros((span, span), F32)
    for chan in range(2):
        line = jnp.sum(taps[chan * half : (chan + 1) * half, :], axis=0, keepdims=True)
        band = pltpu.roll(jnp.broadcast_to(line, (span, span)), 0, 1, stride=1, stride_axis=0)
        band = jnp.where(upper, band, 0.0)
        wide = jnp.concatenate([band, zero] if chan == 0 else [zero, band], axis=1)
        hi, lo = halves(wide)
        band_hi[chan * span : (chan + 1) * span, :] = hi
        band_lo[chan * span : (chan + 1) * span, :] = lo


def skew(value):
    size = value.shape[0]
    sub = lax.broadcasted_iota(jnp.int32, value.shape, 0)
    lane = lax.broadcasted_iota(jnp.int32, value.shape, 1)
    value = jnp.where(lane >= sub, value, 0.0)
    bit = 1
    while bit < size:
        value = jnp.where((sub & bit) != 0, pltpu.roll(value, size - bit, 1), value)
        bit *= 2
    return value


def core_kernel(
    batch,
    recv_ref,
    fwd_hi,
    fwd_lo,
    rev_hi,
    rev_lo,
    mix_hi,
    mix_lo,
    band_hi,
    band_lo,
    prm_ref,
    out_ref,
    rows,
    g_re,
    g_im,
    d_re,
    d_im,
    z_re,
    z_im,
    y_re,
    y_im,
    outs,
):
    sources = rows.shape[0] // ROWS_IN
    chunks = sources // batch
    poles = prm_ref.shape[1]
    span = poles
    half = poles // 2
    rows[...] = recv_ref[...].astype(F32)

    def part(index):
        return rows[pl.ds(index, sources, stride=ROWS_IN), :]

    u_f = jnp.concatenate([part(0), part(1)], axis=1)
    g_f = jnp.concatenate([part(2), part(3)], axis=1)
    u_b, g_b = u_f.astype(BF16), g_f.astype(BF16)
    moments = dot(g_b, fwd_hi[...], FLIP) + dot(g_b, fwd_lo[...], FLIP)
    for index, ref in enumerate((g_re, g_im, d_re, d_im)):
        ref[...] = moments[:, index * poles : (index + 1) * poles]
    prm = prm_ref[...]

    def line(index):
        return prm[index : index + 1, :]

    e_re, e_im = line(0), line(1)
    a, b, c, d = (jnp.zeros((batch, poles), F32) for _ in range(4))
    for chunk in reversed(range(chunks)):
        at = pl.ds(chunk, batch, stride=chunks)
        z_re[at, :] = a
        z_im[at, :] = b
        y_re[at, :] = c
        y_im[at, :] = d
        if chunk > 0:
            m = c + span * a
            n = d + span * b
            a, b = (e_re * a - e_im * b) + g_re[at, :], (e_re * b + e_im * a) + g_im[at, :]
            c, d = (e_re * m - e_im * n) + d_re[at, :], (e_re * n + e_im * m) + d_im[at, :]
    lead = dot(u_b, rev_hi[...], FLIP) + dot(u_b, rev_lo[...], FLIP)
    v_re, v_im = lead[:, :poles], lead[:, poles : 2 * poles]
    x_re, x_im = lead[:, 2 * poles : 3 * poles], lead[:, 3 * poles :]
    a, b, c, d = z_re[...], z_im[...], y_re[...], y_im[...]

    def total(value):
        return jnp.sum(value, axis=0, keepdims=True)

    s_re = total(v_re * a - v_im * b)
    s_im = total(v_re * b + v_im * a)
    t_re = total(x_re * a - x_im * b + v_re * c - v_im * d)
    t_im = total(x_re * b + x_im * a + v_re * d + v_im * c)

    state = jnp.concatenate([a, b], axis=1)
    state_hi, state_lo = halves(state)
    back = dot(state_hi, mix_hi[...], PLAIN) + dot(state_lo, mix_hi[...], PLAIN)
    back = back + dot(state_hi, mix_lo[...], PLAIN)
    back = back + dot(g_b, band_hi[...], FLIP) + dot(g_b, band_lo[...], FLIP)
    gain = jnp.concatenate([line(14), line(15)], axis=1)
    back = back + gain * g_f

    cross = dot(u_b, g_b, OUTER)
    lags = [
        total(skew(cross[k * span : (k + 1) * span, k * span : (k + 1) * span])) for k in range(2)
    ]
    lag = jnp.broadcast_to(jnp.concatenate(lags, axis=1), (8, 2 * span))
    lag_hi, lag_lo = halves(lag)
    near = dot(lag_hi, fwd_hi[...], FLIP) + dot(lag_lo, fwd_hi[...], FLIP)
    near = (near + dot(lag_hi, fwd_lo[...], FLIP))[0:1]
    s_re = s_re + near[:, :poles]
    s_im = s_im + near[:, poles : 2 * poles]
    t_re = t_re + near[:, 2 * poles : 3 * poles]
    t_im = t_im + near[:, 3 * poles :]

    def times(p, q):
        return (p[0] * q[0] - p[1] * q[1], p[0] * q[1] + p[1] * q[0])

    s, t = (s_re, s_im), (t_re, t_im)
    ct, lift = (line(2), line(3)), (line(4), line(5))
    slope, ratio = (line(6), line(7)), (line(8), line(9))
    size, pole_re, w = line(10), line(11), (line(12), line(13))
    by_c = times(s, lift)
    first, second = times(s, slope), times(t, ct)
    by_w = (first[0] + second[0], first[1] + second[1])
    third = times(s, ratio)
    by_a = (size * by_w[0] - third[0], size * by_w[1] - third[1])
    by_dt = 2.0 * (by_w[0] * w[0] - by_w[1] * w[1])
    lane = lax.broadcasted_iota(jnp.int32, (1, poles), 1)
    by_skip = total(u_f * g_f)
    loose = [
        jnp.sum(jnp.where(lane < half, by_dt, 0.0), axis=1, keepdims=True),
        jnp.sum(jnp.where(lane < half, 0.0, by_dt), axis=1, keepdims=True),
        jnp.sum(by_skip[:, :span], axis=1, keepdims=True),
        jnp.sum(by_skip[:, span:], axis=1, keepdims=True),
    ]
    misc = jnp.zeros((1, poles), F32)
    for index, value in enumerate(loose):
        misc = jnp.where(lane == index, value, misc)
    lines = [
        2.0 * by_a[0] * pole_re,
        -2.0 * by_a[1],
        2.0 * by_c[0],
        -2.0 * by_c[1],
        misc,
        jnp.zeros((1, poles), F32),
    ]
    outs[pl.ds(0, sources, stride=ROWS_OUT), :] = back[:, :span]
    outs[pl.ds(1, sources, stride=ROWS_OUT), :] = back[:, span:]
    for index, value in enumerate(lines):
        outs[pl.ds(2 + index, sources, stride=ROWS_OUT), :] = jnp.broadcast_to(
            value, (sources, poles)
        )
    out_ref[...] = outs[...].astype(BF16)


def finish_kernel(recv_ref, grad_ref, a_ref, b_ref, c_ref, d_ref, misc_ref, rows):
    owners = rows.shape[0] // ROWS_OUT
    half = a_ref.shape[0]
    rows[...] = recv_ref[...].astype(F32)

    def turned(index):
        return rows[pl.ds(index, owners, stride=ROWS_OUT), :].T

    for part in range(2):
        grad_ref[:, part * owners : (part + 1) * owners] = turned(part).astype(BF16)
    for index, ref in enumerate((a_ref, b_ref, c_ref, d_ref)):
        block = turned(2 + index)
        ref[:, :owners] = block[:half]
        ref[:, owners:] = block[half:]
    misc_ref[...] = turned(6)[0:8]


def pole_lines(step_size, pole_re, a_im, c_re, c_im):
    w_re = step_size * pole_re
    w_im = step_size * a_im
    growth = jnp.exp(w_re)
    cosine, sine = jnp.cos(w_im), jnp.sin(w_im)
    half_sin = jnp.sin(0.5 * w_im)
    e_re = jnp.expm1(w_re) * cosine - 2.0 * half_sin * half_sin
    e_im = growth * sine
    modulus = pole_re * pole_re + a_im * a_im

    def over_pole(re, im):
        return ((re * pole_re + im * a_im) / modulus, (im * pole_re - re * a_im) / modulus)

    ct_re, ct_im = over_pole(e_re * c_re - e_im * c_im, e_re * c_im + e_im * c_re)
    lift = over_pole(e_re, e_im)
    g_re, g_im = growth * cosine, growth * sine
    slope = over_pole(g_re * c_re - g_im * c_im, g_re * c_im + g_im * c_re)
    ratio = over_pole(ct_re, ct_im)
    return (w_re, w_im, ct_re, ct_im) + lift + slope + ratio


def vmem(count):
    return [pl.BlockSpec(memory_space=pltpu.VMEM)] * count


def body(inputs, grad_out, log_dt, log_a_re, a_im, c_re, c_im, skip_gain):
    batch = lax.axis_size("dp")
    devices = batch * lax.axis_size("ctx")
    span, channels = inputs.shape[1:]
    poles = a_im.shape[1]
    assert channels == 2 * devices and span == 2 * poles
    place = lax.axis_index(AXES)

    sent = pl.pallas_call(
        send_kernel,
        out_shape=jax.ShapeDtypeStruct((devices * ROWS_IN, span), BF16),
        in_specs=vmem(2),
        out_specs=vmem(1)[0],
        scratch_shapes=[pltpu.VMEM((devices * ROWS_IN, span), F32)],
    )(inputs[0], grad_out[0])
    recv = lax.all_to_all(
        sent.reshape(devices, ROWS_IN, span), AXES, split_axis=0, concat_axis=0, tiled=True
    ).reshape(devices * ROWS_IN, span)

    def own(value):
        turned = value.T
        pair = [
            lax.dynamic_slice_in_dim(turned, place + k * devices, 1, axis=1) for k in range(2)
        ]
        return jnp.concatenate(pair, axis=0)[:, 0]

    def own_flat(value):
        pair = [lax.dynamic_slice_in_dim(value, place + k * devices, 1) for k in range(2)]
        return jnp.repeat(jnp.concatenate(pair), poles)

    step_size = jnp.exp(own_flat(log_dt))
    pole_re = -jnp.exp(own(log_a_re))
    im = own(a_im)
    terms = pole_lines(step_size, pole_re, im, own(c_re), own(c_im))
    w_re, w_im, ct_re, ct_im = terms[:4]
    far = jnp.exp(w_re * span)
    gains = [
        jnp.broadcast_to(lax.dynamic_slice_in_dim(skip_gain, place + k * devices, 1), (span,))
        for k in range(2)
    ]
    prm = jnp.stack(
        [far * jnp.cos(w_im * span), far * jnp.sin(w_im * span)]
        + list(terms[2:])
        + [step_size, pole_re, w_re, w_im]
        + gains
    )
    cols = jnp.stack([w_re, w_im, ct_re, ct_im], axis=1)
    wide = 2 * span
    tall = jax.ShapeDtypeStruct((4 * 2 * poles, wide), BF16)
    square = jax.ShapeDtypeStruct((wide, wide), BF16)
    tables = pl.pallas_call(
        table_kernel,
        out_shape=[tall] * 4 + [square] * 4,
        in_specs=vmem(1),
        out_specs=vmem(8),
    )(cols)
    grid = pltpu.VMEM((devices, span), F32)
    answer = pl.pallas_call(
        functools.partial(core_kernel, batch),
        out_shape=jax.ShapeDtypeStruct((devices * ROWS_OUT, span), BF16),
        in_specs=vmem(10),
        out_specs=vmem(1)[0],
        scratch_shapes=[pltpu.VMEM((devices * ROWS_IN, span), F32)]
        + [grid] * 8
        + [pltpu.VMEM((devices * ROWS_OUT, span), F32)],
    )(recv, *tables, prm)
    back = lax.all_to_all(
        answer.reshape(devices, ROWS_OUT, span), AXES, split_axis=0, concat_axis=0, tiled=True
    ).reshape(devices * ROWS_OUT, span)
    line = jax.ShapeDtypeStruct((poles, channels), F32)
    results = pl.pallas_call(
        finish_kernel,
        out_shape=[jax.ShapeDtypeStruct((span, channels), BF16)]
        + [line] * 4
        + [jax.ShapeDtypeStruct((8, devices), F32)],
        in_specs=vmem(1),
        out_specs=vmem(6),
        scratch_shapes=[pltpu.VMEM((devices * ROWS_OUT, span), F32)],
    )(back)
    misc = results[5]
    return (
        results[0][None],
        misc[0:2].reshape(channels),
        results[1].T,
        results[2].T,
        results[3].T,
        results[4].T,
        misc[2:4].reshape(channels),
    )


def solution(mesh):
    placed = (P("dp", "ctx", None), P("dp", "ctx", None), P(), P(), P(), P(), P(), P())
    return jax.shard_map(
        body,
        mesh=mesh,
        in_specs=placed,
        out_specs=(P("dp", "ctx", None), P(), P(), P(), P(), P(), P()),
        check_vma=False,
    )
```

```python
import functools

import jax
import jax.numpy as jnp
from jax import lax
from jax.experimental import pallas as pl
from jax.experimental.pallas import tpu as pltpu
from jax.sharding import Mesh
from jax.sharding import PartitionSpec as P

OWNER = ("core", "dpair", "ctx")
CHIP = ("dpair", "ctx")
F32 = jnp.float32
BF16 = jnp.bfloat16
ROWS_IN = 4
ROWS_OUT = 10
LIMIT = pltpu.CompilerParams(vmem_limit_bytes=16 * 1024 * 1024)
FLIP = (((1,), (1,)), ((), ()))
PLAIN = (((1,), (0,)), ((), ()))
OUTER = (((0,), (0,)), ((), ()))


def halves(value):
    high = value.astype(BF16)
    low = (value - high.astype(F32)).astype(BF16)
    return (high, low)


def dot(a, b, dims):
    return lax.dot_general(a, b, dims, preferred_element_type=F32)


def send_kernel(inputs_ref, grad_ref, out_ref, rows):
    owners = rows.shape[0] // ROWS_IN
    for part, ref in enumerate((inputs_ref, grad_ref)):
        block = ref[...].astype(F32)
        for half in range(2):
            piece = block[:, half * owners : (half + 1) * owners].T
            rows[pl.ds(2 * part + half, owners, stride=ROWS_IN), :] = piece
    out_ref[...] = rows[...].astype(BF16)


def table_kernel(cols_ref, fwd_hi, fwd_lo, rev_hi, rev_lo, mix_hi, mix_lo, band_hi, band_lo):
    poles = cols_ref.shape[0]
    half = poles // 2
    span = poles
    w_re, w_im = cols_ref[:, 0:1], cols_ref[:, 1:2]
    ct_re, ct_im = cols_ref[:, 2:3], cols_ref[:, 3:4]
    lane = lax.broadcasted_iota(jnp.int32, (poles, span), 1)
    sub = lax.broadcasted_iota(jnp.int32, (poles, span), 0)
    first = sub < half

    def spread(value):
        return jnp.concatenate([jnp.where(first, value, 0.0), jnp.where(first, 0.0, value)], axis=1)

    def put(hi_ref, lo_ref, part, value):
        hi, lo = halves(spread(value))
        hi_ref[part * poles : (part + 1) * poles, :] = hi
        lo_ref[part * poles : (part + 1) * poles, :] = lo

    step = lane.astype(F32)
    grow = jnp.exp(w_re * step)
    turn = w_im * step
    f_re, f_im = grow * jnp.cos(turn), grow * jnp.sin(turn)
    put(fwd_hi, fwd_lo, 0, f_re)
    put(fwd_hi, fwd_lo, 1, f_im)
    put(fwd_hi, fwd_lo, 2, f_re * step)
    put(fwd_hi, fwd_lo, 3, f_im * step)
    back = (span - lane).astype(F32)
    shrink = jnp.exp(w_re * back)
    twist = w_im * back
    h_re, h_im = shrink * jnp.cos(twist), shrink * jnp.sin(twist)
    put(rev_hi, rev_lo, 0, h_re)
    put(rev_hi, rev_lo, 1, h_im)
    put(rev_hi, rev_lo, 2, h_re * back)
    put(rev_hi, rev_lo, 3, h_im * back)
    put(mix_hi, mix_lo, 0, 2.0 * (ct_re * h_re - ct_im * h_im))
    put(mix_hi, mix_lo, 1, -2.0 * (ct_re * h_im + ct_im * h_re))
    taps = 2.0 * (ct_re * f_re - ct_im * f_im)
    upper = lane >= sub
    zero = jnp.zeros((span, span), F32)
    for chan in range(2):
        line = jnp.sum(taps[chan * half : (chan + 1) * half, :], axis=0, keepdims=True)
        band = pltpu.roll(jnp.broadcast_to(line, (span, span)), 0, 1, stride=1, stride_axis=0)
        band = jnp.where(upper, band, 0.0)
        wide = jnp.concatenate([band, zero] if chan == 0 else [zero, band], axis=1)
        hi, lo = halves(wide)
        band_hi[chan * span : (chan + 1) * span, :] = hi
        band_lo[chan * span : (chan + 1) * span, :] = lo


def skew(value):
    size = value.shape[0]
    sub = lax.broadcasted_iota(jnp.int32, value.shape, 0)
    lane = lax.broadcasted_iota(jnp.int32, value.shape, 1)
    value = jnp.where(lane >= sub, value, 0.0)
    bit = 1
    while bit < size:
        value = jnp.where((sub & bit) != 0, pltpu.roll(value, size - bit, 1), value)
        bit *= 2
    return value


def core_kernel(
    batch,
    recv_ref,
    fwd_hi,
    fwd_lo,
    rev_hi,
    rev_lo,
    mix_hi,
    mix_lo,
    band_hi,
    band_lo,
    prm_ref,
    out_ref,
    rows,
    g_re,
    g_im,
    d_re,
    d_im,
    z_re,
    z_im,
    y_re,
    y_im,
    outs,
):
    sources = rows.shape[0] // ROWS_IN
    chunks = sources // batch
    poles = prm_ref.shape[1]
    span = poles
    half = poles // 2
    rows[...] = recv_ref[...].astype(F32)

    def part(index):
        return rows[pl.ds(index, sources, stride=ROWS_IN), :]

    u_f = jnp.concatenate([part(0), part(1)], axis=1)
    g_f = jnp.concatenate([part(2), part(3)], axis=1)
    u_b, g_b = u_f.astype(BF16), g_f.astype(BF16)
    moments = dot(g_b, fwd_hi[...], FLIP) + dot(g_b, fwd_lo[...], FLIP)
    for index, ref in enumerate((g_re, g_im, d_re, d_im)):
        ref[...] = moments[:, index * poles : (index + 1) * poles]
    prm = prm_ref[...]

    def line(index):
        return prm[index : index + 1, :]

    e_re, e_im = line(0), line(1)
    a, b, c, d = (jnp.zeros((batch, poles), F32) for _ in range(4))
    for chunk in reversed(range(chunks)):
        at = pl.ds(chunk, batch, stride=chunks)
        z_re[at, :] = a
        z_im[at, :] = b
        y_re[at, :] = c
        y_im[at, :] = d
        if chunk > 0:
            m = c + span * a
            n = d + span * b
            a, b = (e_re * a - e_im * b) + g_re[at, :], (e_re * b + e_im * a) + g_im[at, :]
            c, d = (e_re * m - e_im * n) + d_re[at, :], (e_re * n + e_im * m) + d_im[at, :]
    lead = dot(u_b, rev_hi[...], FLIP) + dot(u_b, rev_lo[...], FLIP)
    v_re, v_im = lead[:, :poles], lead[:, poles : 2 * poles]
    x_re, x_im = lead[:, 2 * poles : 3 * poles], lead[:, 3 * poles :]
    a, b, c, d = z_re[...], z_im[...], y_re[...], y_im[...]

    def total(value):
        return jnp.sum(value, axis=0, keepdims=True)

    s_re = total(v_re * a - v_im * b)
    s_im = total(v_re * b + v_im * a)
    t_re = total(x_re * a - x_im * b + v_re * c - v_im * d)
    t_im = total(x_re * b + x_im * a + v_re * d + v_im * c)

    state = jnp.concatenate([a, b], axis=1)
    state_hi, state_lo = halves(state)
    back = dot(state_hi, mix_hi[...], PLAIN) + dot(state_lo, mix_hi[...], PLAIN)
    back = back + dot(state_hi, mix_lo[...], PLAIN)
    back = back + dot(g_b, band_hi[...], FLIP) + dot(g_b, band_lo[...], FLIP)
    gain = jnp.concatenate([line(14), line(15)], axis=1)
    back = back + gain * g_f

    cross = dot(u_b, g_b, OUTER)
    lags = [
        total(skew(cross[k * span : (k + 1) * span, k * span : (k + 1) * span])) for k in range(2)
    ]
    lag = jnp.broadcast_to(jnp.concatenate(lags, axis=1), (8, 2 * span))
    lag_hi, lag_lo = halves(lag)
    near = dot(lag_hi, fwd_hi[...], FLIP) + dot(lag_lo, fwd_hi[...], FLIP)
    near = (near + dot(lag_hi, fwd_lo[...], FLIP))[0:1]
    s_re = s_re + near[:, :poles]
    s_im = s_im + near[:, poles : 2 * poles]
    t_re = t_re + near[:, 2 * poles : 3 * poles]
    t_im = t_im + near[:, 3 * poles :]

    def times(p, q):
        return (p[0] * q[0] - p[1] * q[1], p[0] * q[1] + p[1] * q[0])

    s, t = (s_re, s_im), (t_re, t_im)
    ct, lift = (line(2), line(3)), (line(4), line(5))
    slope, ratio = (line(6), line(7)), (line(8), line(9))
    size, pole_re, w = line(10), line(11), (line(12), line(13))
    by_c = times(s, lift)
    first, second = times(s, slope), times(t, ct)
    by_w = (first[0] + second[0], first[1] + second[1])
    third = times(s, ratio)
    by_a = (size * by_w[0] - third[0], size * by_w[1] - third[1])
    by_dt = 2.0 * (by_w[0] * w[0] - by_w[1] * w[1])
    lane = lax.broadcasted_iota(jnp.int32, (1, poles), 1)
    by_skip = total(u_f * g_f)
    loose = [
        jnp.sum(jnp.where(lane < half, by_dt, 0.0), axis=1, keepdims=True),
        jnp.sum(jnp.where(lane < half, 0.0, by_dt), axis=1, keepdims=True),
        jnp.sum(by_skip[:, :span], axis=1, keepdims=True),
        jnp.sum(by_skip[:, span:], axis=1, keepdims=True),
    ]
    misc = jnp.zeros((1, poles), F32)
    for index, value in enumerate(loose):
        misc = jnp.where(lane == index, value, misc)
    lines = [
        2.0 * by_a[0] * pole_re,
        -2.0 * by_a[1],
        2.0 * by_c[0],
        -2.0 * by_c[1],
        misc,
        jnp.zeros((1, poles), F32),
    ]
    chips = sources // 2
    for core in range(2):
        for chan in range(2):
            outs[pl.ds(2 * core + chan, chips, stride=ROWS_OUT), :] = back[
                core * chips : (core + 1) * chips, chan * span : (chan + 1) * span
            ]
    for index, value in enumerate(lines):
        outs[pl.ds(4 + index, chips, stride=ROWS_OUT), :] = jnp.broadcast_to(value, (chips, poles))
    out_ref[...] = outs[...].astype(BF16)


def finish_kernel(core_ref, mine_ref, other_ref, grad_ref, a_ref, b_ref, c_ref, d_ref, dt_ref, skip_ref, rows):
    chips = rows.shape[1] // ROWS_OUT
    half = a_ref.shape[0]
    core = core_ref[0]
    rows[core] = mine_ref[...].astype(F32)
    rows[1 - core] = other_ref[...].astype(F32)

    def turned(owner, index):
        return rows[owner, pl.ds(index, chips, stride=ROWS_OUT), :].T

    for owner in range(2):
        for chan in range(2):
            at = (2 * chan + owner) * chips
            grad_ref[:, at : at + chips] = turned(owner, 2 * core + chan).astype(BF16)
        for index, ref in enumerate((a_ref, b_ref, c_ref, d_ref)):
            block = turned(owner, 4 + index)
            for chan in range(2):
                at = (2 * chan + owner) * chips
                ref[:, at : at + chips] = block[chan * half : (chan + 1) * half]
        misc = turned(owner, 8)
        for chan in range(2):
            at = (2 * chan + owner) * chips
            dt_ref[:, at : at + chips] = misc[chan : chan + 1]
            skip_ref[:, at : at + chips] = misc[2 + chan : 3 + chan]


def pole_lines(step_size, pole_re, a_im, c_re, c_im):
    w_re = step_size * pole_re
    w_im = step_size * a_im
    growth = jnp.exp(w_re)
    cosine, sine = jnp.cos(w_im), jnp.sin(w_im)
    half_sin = jnp.sin(0.5 * w_im)
    e_re = jnp.expm1(w_re) * cosine - 2.0 * half_sin * half_sin
    e_im = growth * sine
    modulus = pole_re * pole_re + a_im * a_im

    def over_pole(re, im):
        return ((re * pole_re + im * a_im) / modulus, (im * pole_re - re * a_im) / modulus)

    ct_re, ct_im = over_pole(e_re * c_re - e_im * c_im, e_re * c_im + e_im * c_re)
    lift = over_pole(e_re, e_im)
    g_re, g_im = growth * cosine, growth * sine
    slope = over_pole(g_re * c_re - g_im * c_im, g_re * c_im + g_im * c_re)
    ratio = over_pole(ct_re, ct_im)
    return (w_re, w_im, ct_re, ct_im) + lift + slope + ratio


def vmem(count):
    return [pl.BlockSpec(memory_space=pltpu.VMEM)] * count


def body(inputs, grad_out, log_dt, log_a_re, a_im, c_re, c_im, skip_gain):
    batch = lax.axis_size("dpair") * lax.axis_size("core")
    devices = batch * lax.axis_size("ctx")
    span, channels = inputs.shape[1:]
    poles = a_im.shape[1]
    assert channels == 2 * devices and span == 2 * poles
    place = lax.axis_index(OWNER)

    sent = pl.pallas_call(
        send_kernel,
        out_shape=jax.ShapeDtypeStruct((devices * ROWS_IN, span), BF16),
        in_specs=vmem(2),
        out_specs=vmem(1)[0],
        scratch_shapes=[pltpu.VMEM((devices * ROWS_IN, span), F32)],
        compiler_params=LIMIT,
    )(inputs[0], grad_out[0])
    recv = lax.all_to_all(
        sent.reshape(devices, ROWS_IN, span), OWNER, split_axis=0, concat_axis=0, tiled=True
    ).reshape(devices * ROWS_IN, span)

    def own(value):
        turned = value.T
        pair = [
            lax.dynamic_slice_in_dim(turned, place + k * devices, 1, axis=1) for k in range(2)
        ]
        return jnp.concatenate(pair, axis=0)[:, 0]

    def own_flat(value):
        pair = [lax.dynamic_slice_in_dim(value, place + k * devices, 1) for k in range(2)]
        return jnp.repeat(jnp.concatenate(pair), poles)

    step_size = jnp.exp(own_flat(log_dt))
    pole_re = -jnp.exp(own(log_a_re))
    im = own(a_im)
    terms = pole_lines(step_size, pole_re, im, own(c_re), own(c_im))
    w_re, w_im, ct_re, ct_im = terms[:4]
    far = jnp.exp(w_re * span)
    gains = [
        jnp.broadcast_to(lax.dynamic_slice_in_dim(skip_gain, place + k * devices, 1), (span,))
        for k in range(2)
    ]
    prm = jnp.stack(
        [far * jnp.cos(w_im * span), far * jnp.sin(w_im * span)]
        + list(terms[2:])
        + [step_size, pole_re, w_re, w_im]
        + gains
    )
    cols = jnp.stack([w_re, w_im, ct_re, ct_im], axis=1)
    wide = 2 * span
    tall = jax.ShapeDtypeStruct((4 * 2 * poles, wide), BF16)
    square = jax.ShapeDtypeStruct((wide, wide), BF16)
    tables = pl.pallas_call(
        table_kernel,
        out_shape=[tall] * 4 + [square] * 4,
        in_specs=vmem(1),
        out_specs=vmem(8),
        compiler_params=LIMIT,
    )(cols)
    grid = pltpu.VMEM((devices, span), F32)
    chips = devices // 2
    answer = pl.pallas_call(
        functools.partial(core_kernel, batch),
        out_shape=jax.ShapeDtypeStruct((chips * ROWS_OUT, span), BF16),
        in_specs=vmem(10),
        out_specs=vmem(1)[0],
        scratch_shapes=[pltpu.VMEM((devices * ROWS_IN, span), F32)]
        + [grid] * 8
        + [pltpu.VMEM((chips * ROWS_OUT, span), F32)],
        compiler_params=LIMIT,
    )(recv, *tables, prm)
    mine = lax.all_to_all(
        answer.reshape(chips, ROWS_OUT // 2, 2, span), CHIP, split_axis=0, concat_axis=0, tiled=True
    ).reshape(chips * ROWS_OUT, span)
    other = lax.ppermute(mine, "core", [(0, 1), (1, 0)])
    line = jax.ShapeDtypeStruct((poles, channels), F32)
    single = jax.ShapeDtypeStruct((1, channels), F32)
    results = pl.pallas_call(
        finish_kernel,
        out_shape=[jax.ShapeDtypeStruct((span, channels), BF16)] + [line] * 4 + [single] * 2,
        in_specs=[pl.BlockSpec(memory_space=pltpu.SMEM)] + vmem(2),
        out_specs=vmem(7),
        scratch_shapes=[pltpu.VMEM((2, chips * ROWS_OUT, span), F32)],
        compiler_params=LIMIT,
    )(lax.axis_index("core").reshape(1), mine, other)
    return (
        results[0][None],
        results[5].reshape(channels),
        results[1].T,
        results[2].T,
        results[3].T,
        results[4].T,
        results[6].reshape(channels),
    )


def solution(mesh):
    pairs, ctx = mesh.devices.shape[0] // 2, mesh.devices.shape[1]
    fine = Mesh(mesh.devices.reshape(pairs, 2, ctx), ("dpair", "core", "ctx"))
    block = P(("dpair", "core"), "ctx", None)
    return jax.shard_map(
        body,
        mesh=fine,
        in_specs=(block, block, P(), P(), P(), P(), P(), P()),
        out_specs=(block, P(), P(), P(), P(), P(), P()),
        check_vma=False,
    )
```

```python
import functools

import jax
import jax.numpy as jnp
from jax import lax
from jax.experimental import pallas as pl
from jax.experimental.pallas import tpu as pltpu
from jax.sharding import Mesh
from jax.sharding import PartitionSpec as P

OWNER = ("ctx", "dpair", "core")
CHIP = ("ctx", "dpair")
F32 = jnp.float32
BF16 = jnp.bfloat16
ROWS_IN = 4
ROWS_OUT = 10
SEND_PIECES = 4
EVERY = 8
LIMIT = pltpu.CompilerParams(vmem_limit_bytes=16 * 1024 * 1024)
FLIP = (((1,), (1,)), ((), ()))
PLAIN = (((1,), (0,)), ((), ()))
OUTER = (((0,), (0,)), ((), ()))


def halves(value):
    high = value.astype(BF16)
    low = (value - high.astype(F32)).astype(BF16)
    return (high, low)


def dot(a, b, dims):
    return lax.dot_general(a, b, dims, preferred_element_type=F32)


def send_kernel(inputs_ref, grad_ref, out_ref, stage, rows, packed, sems):
    owners = rows.shape[0] // ROWS_IN
    chips = owners // 2
    loads = [
        pltpu.make_async_copy(ref, stage.at[part], sems.at[part])
        for part, ref in enumerate((inputs_ref, grad_ref))
    ]
    for load in loads:
        load.start()
    for part, load in enumerate(loads):
        load.wait()
        for half in range(2):
            for core in range(2):
                at = half * owners + core * chips
                piece = stage[part, :, at : at + chips].astype(F32).T
                line = ROWS_IN * core + 2 * part + half
                rows[pl.ds(line, chips, stride=2 * ROWS_IN), :] = piece
    pieces = sems.shape[0] - 2
    size = rows.shape[0] // pieces
    stores = []
    for index in range(pieces):
        at = pl.ds(index * size, size)
        packed[at, :] = rows[at, :].astype(BF16)
        stores.append(pltpu.make_async_copy(packed.at[at, :], out_ref.at[at, :], sems.at[2 + index]))
        stores[-1].start()
    for store in stores:
        store.wait()


def table_kernel(cols_ref, fwd_hi, fwd_lo, rev_hi, rev_lo, mix_hi, mix_lo, band_hi, band_lo, flip_ref):
    poles = cols_ref.shape[0]
    half = poles // 2
    span = poles
    w_re, w_im = cols_ref[:, 0:1], cols_ref[:, 1:2]
    ct_re, ct_im = cols_ref[:, 2:3], cols_ref[:, 3:4]
    lane = lax.broadcasted_iota(jnp.int32, (poles, span), 1)
    sub = lax.broadcasted_iota(jnp.int32, (poles, span), 0)
    first = sub < half

    def spread(value):
        return jnp.concatenate([jnp.where(first, value, 0.0), jnp.where(first, 0.0, value)], axis=1)

    def put(hi_ref, lo_ref, part, value):
        hi, lo = halves(spread(value))
        hi_ref[part * poles : (part + 1) * poles, :] = hi
        lo_ref[part * poles : (part + 1) * poles, :] = lo

    step = lane.astype(F32)
    grow = jnp.exp(w_re * step)
    turn = w_im * step
    f_re, f_im = grow * jnp.cos(turn), grow * jnp.sin(turn)
    put(fwd_hi, fwd_lo, 0, f_re)
    put(fwd_hi, fwd_lo, 1, f_im)
    put(fwd_hi, fwd_lo, 2, f_re * step)
    put(fwd_hi, fwd_lo, 3, f_im * step)
    back = (span - lane).astype(F32)
    shrink = jnp.exp(w_re * back)
    twist = w_im * back
    h_re, h_im = shrink * jnp.cos(twist), shrink * jnp.sin(twist)
    put(rev_hi, rev_lo, 0, h_re)
    put(rev_hi, rev_lo, 1, h_im)
    put(rev_hi, rev_lo, 2, h_re * back)
    put(rev_hi, rev_lo, 3, h_im * back)
    put(mix_hi, mix_lo, 0, 2.0 * (ct_re * h_re - ct_im * h_im))
    put(mix_hi, mix_lo, 1, -2.0 * (ct_re * h_im + ct_im * h_re))
    taps = 2.0 * (ct_re * f_re - ct_im * f_im)
    upper = lane >= sub
    zero = jnp.zeros((span, span), F32)
    for chan in range(2):
        line = jnp.sum(taps[chan * half : (chan + 1) * half, :], axis=0, keepdims=True)
        band = pltpu.roll(jnp.broadcast_to(line, (span, span)), 0, 1, stride=1, stride_axis=0)
        band = jnp.where(upper, band, 0.0)
        wide = jnp.concatenate([band, zero] if chan == 0 else [zero, band], axis=1)
        hi, lo = halves(wide)
        band_hi[chan * span : (chan + 1) * span, :] = hi
        band_lo[chan * span : (chan + 1) * span, :] = lo
    wide_sub = lax.broadcasted_iota(jnp.int32, flip_ref.shape, 0)
    wide_lane = lax.broadcasted_iota(jnp.int32, flip_ref.shape, 1)
    same = (wide_sub < span) == (wide_lane < span)
    mirror = (wide_sub % span) + (wide_lane % span) == span - 1
    flip_ref[...] = jnp.where(same & mirror, 1.0, 0.0).astype(BF16)


def diagonals(value):
    sub = lax.broadcasted_iota(jnp.int32, value.shape, 0)
    lane = lax.broadcasted_iota(jnp.int32, value.shape, 1)
    value = jnp.where(lane + sub >= value.shape[0] - 1, value, 0.0)
    return pltpu.roll(value, 1, 1, stride=1, stride_axis=0)


def core_kernel(
    batch,
    recv_ref,
    fwd_hi,
    fwd_lo,
    rev_hi,
    rev_lo,
    mix_hi,
    mix_lo,
    band_hi,
    band_lo,
    flip_ref,
    prm_ref,
    out_ref,
    rows,
    g_re,
    g_im,
    d_re,
    d_im,
    z_re,
    z_im,
    v_re,
    v_im,
    x_re,
    x_im,
    base,
    outs,
):
    sources = rows.shape[0] // ROWS_IN
    chunks = sources // batch
    poles = prm_ref.shape[1]
    span = poles
    half = poles // 2
    rows[...] = recv_ref[...].astype(F32)

    def part(index):
        return rows[pl.ds(index, sources, stride=ROWS_IN), :]

    u_f = jnp.concatenate([part(0), part(1)], axis=1)
    g_f = jnp.concatenate([part(2), part(3)], axis=1)
    u_b, g_b = u_f.astype(BF16), g_f.astype(BF16)
    moments = dot(g_b, fwd_hi[...], FLIP) + dot(g_b, fwd_lo[...], FLIP)
    for index, ref in enumerate((g_re, g_im, d_re, d_im)):
        ref[...] = moments[:, index * poles : (index + 1) * poles]
    lead = dot(u_b, rev_hi[...], FLIP) + dot(u_b, rev_lo[...], FLIP)
    for index, ref in enumerate((v_re, v_im, x_re, x_im)):
        ref[...] = lead[:, index * poles : (index + 1) * poles]
    prm = prm_ref[...]

    def line(index):
        return prm[index : index + 1, :]

    def total(value):
        return jnp.sum(value, axis=0, keepdims=True)

    e_re, e_im = line(0), line(1)
    gain = jnp.concatenate([line(14), line(15)], axis=1)
    near = []
    flipped = []
    cross = []

    def flip():
        flipped.append(dot(u_b, flip_ref[...], PLAIN).astype(BF16))

    def correlate():
        cross.append(dot(flipped[0], g_b, OUTER))

    def gather():
        parts = [cross[0][k * span : (k + 1) * span, k * span : (k + 1) * span] for k in range(2)]
        lag = jnp.concatenate([total(diagonals(value)) for value in parts], axis=1)
        lag_hi, lag_lo = halves(jnp.broadcast_to(lag, (8, 2 * span)))
        value = dot(lag_hi, fwd_hi[...], FLIP) + dot(lag_lo, fwd_hi[...], FLIP)
        near.append((value + dot(lag_hi, fwd_lo[...], FLIP))[0:1])

    def local(at):
        g_rows = g_b[at : at + span]
        value = dot(g_rows, band_hi[...], FLIP) + dot(g_rows, band_lo[...], FLIP)
        value = value + gain * g_f[at : at + span]
        for chan in range(2):
            base[chan, at : at + span, :] = value[:, chan * span : (chan + 1) * span]

    tasks = [flip, correlate, gather]
    tasks += [functools.partial(local, at) for at in range(0, sources, span)]
    a, b, c, d, s_re, s_im, t_re, t_im = (jnp.zeros((batch, poles), F32) for _ in range(8))
    for chunk in reversed(range(chunks)):
        at = pl.ds(chunk * batch, batch)
        z_re[at, :] = a
        z_im[at, :] = b
        if chunk < chunks - 1:
            p, q, x, y = v_re[at, :], v_im[at, :], x_re[at, :], x_im[at, :]
            s_re, s_im = s_re + (p * a - q * b), s_im + (p * b + q * a)
            t_re = t_re + (x * a - y * b) + (p * c - q * d)
            t_im = t_im + (x * b + y * a) + (p * d + q * c)
        if chunk > 0:
            m = c + span * a
            n = d + span * b
            a, b = (e_re * a - e_im * b) + g_re[at, :], (e_re * b + e_im * a) + g_im[at, :]
            c, d = (e_re * m - e_im * n) + d_re[at, :], (e_re * n + e_im * m) + d_im[at, :]
        if chunk % EVERY == 0 and tasks:
            tasks.pop(0)()
    for task in tasks:
        task()
    near = near[0]
    s_re, s_im, t_re, t_im = total(s_re), total(s_im), total(t_re), total(t_im)

    state = jnp.concatenate([z_re[...], z_im[...]], axis=1)
    state_hi, state_lo = halves(state)
    back = dot(state_hi, mix_hi[...], PLAIN) + dot(state_lo, mix_hi[...], PLAIN)
    back = back + dot(state_hi, mix_lo[...], PLAIN)
    for chan in range(2):
        base[chan] = base[chan] + back[:, chan * span : (chan + 1) * span]

    s_re = s_re + near[:, :poles]
    s_im = s_im + near[:, poles : 2 * poles]
    t_re = t_re + near[:, 2 * poles : 3 * poles]
    t_im = t_im + near[:, 3 * poles :]

    def times(p, q):
        return (p[0] * q[0] - p[1] * q[1], p[0] * q[1] + p[1] * q[0])

    s, t = (s_re, s_im), (t_re, t_im)
    ct, lift = (line(2), line(3)), (line(4), line(5))
    slope, ratio = (line(6), line(7)), (line(8), line(9))
    size, pole_re, w = line(10), line(11), (line(12), line(13))
    by_c = times(s, lift)
    first, second = times(s, slope), times(t, ct)
    by_w = (first[0] + second[0], first[1] + second[1])
    third = times(s, ratio)
    by_a = (size * by_w[0] - third[0], size * by_w[1] - third[1])
    by_dt = 2.0 * (by_w[0] * w[0] - by_w[1] * w[1])
    lane = lax.broadcasted_iota(jnp.int32, (1, poles), 1)
    by_skip = total(u_f * g_f)
    loose = [
        jnp.sum(jnp.where(lane < half, by_dt, 0.0), axis=1, keepdims=True),
        jnp.sum(jnp.where(lane < half, 0.0, by_dt), axis=1, keepdims=True),
        jnp.sum(by_skip[:, :span], axis=1, keepdims=True),
        jnp.sum(by_skip[:, span:], axis=1, keepdims=True),
    ]
    misc = jnp.zeros((1, poles), F32)
    for index, value in enumerate(loose):
        misc = jnp.where(lane == index, value, misc)
    lines = [
        2.0 * by_a[0] * pole_re,
        -2.0 * by_a[1],
        2.0 * by_c[0],
        -2.0 * by_c[1],
        misc,
        jnp.zeros((1, poles), F32),
    ]
    chips = sources // 2
    for core in range(2):
        for chan in range(2):
            outs[pl.ds(2 * core + chan, chips, stride=ROWS_OUT), :] = base[
                chan, pl.ds(core, chips, stride=2), :
            ]
    for index, value in enumerate(lines):
        outs[pl.ds(4 + index, chips, stride=ROWS_OUT), :] = jnp.broadcast_to(value, (chips, poles))
    out_ref[...] = outs[...].astype(BF16)


def finish_kernel(core_ref, mine_ref, other_ref, grad_ref, a_ref, b_ref, c_ref, d_ref, dt_ref, skip_ref, rows):
    chips = rows.shape[1] // ROWS_OUT
    half = a_ref.shape[0]
    core = core_ref[0]
    rows[core] = mine_ref[...].astype(F32)
    rows[1 - core] = other_ref[...].astype(F32)

    def turned(owner, index):
        return rows[owner, pl.ds(index, chips, stride=ROWS_OUT), :].T

    for owner in range(2):
        for chan in range(2):
            at = (2 * chan + owner) * chips
            grad_ref[:, at : at + chips] = turned(owner, 2 * core + chan).astype(BF16)
        for index, ref in enumerate((a_ref, b_ref, c_ref, d_ref)):
            block = turned(owner, 4 + index)
            for chan in range(2):
                at = (2 * chan + owner) * chips
                ref[:, at : at + chips] = block[chan * half : (chan + 1) * half]
        misc = turned(owner, 8)
        for chan in range(2):
            at = (2 * chan + owner) * chips
            dt_ref[:, at : at + chips] = misc[chan : chan + 1]
            skip_ref[:, at : at + chips] = misc[2 + chan : 3 + chan]


def pole_lines(step_size, pole_re, a_im, c_re, c_im):
    w_re = step_size * pole_re
    w_im = step_size * a_im
    growth = jnp.exp(w_re)
    cosine, sine = jnp.cos(w_im), jnp.sin(w_im)
    half_sin = jnp.sin(0.5 * w_im)
    e_re = jnp.expm1(w_re) * cosine - 2.0 * half_sin * half_sin
    e_im = growth * sine
    modulus = pole_re * pole_re + a_im * a_im

    def over_pole(re, im):
        return ((re * pole_re + im * a_im) / modulus, (im * pole_re - re * a_im) / modulus)

    ct_re, ct_im = over_pole(e_re * c_re - e_im * c_im, e_re * c_im + e_im * c_re)
    lift = over_pole(e_re, e_im)
    g_re, g_im = growth * cosine, growth * sine
    slope = over_pole(g_re * c_re - g_im * c_im, g_re * c_im + g_im * c_re)
    ratio = over_pole(ct_re, ct_im)
    return (w_re, w_im, ct_re, ct_im) + lift + slope + ratio


def vmem(count):
    return [pl.BlockSpec(memory_space=pltpu.VMEM)] * count


def body(inputs, grad_out, log_dt, log_a_re, a_im, c_re, c_im, skip_gain):
    batch = lax.axis_size("dpair") * lax.axis_size("core")
    devices = batch * lax.axis_size("ctx")
    span, channels = inputs.shape[1:]
    poles = a_im.shape[1]
    assert channels == 2 * devices and span == 2 * poles
    chips = devices // 2
    place = lax.axis_index("core") * chips + lax.axis_index(CHIP)

    sent = pl.pallas_call(
        send_kernel,
        out_shape=jax.ShapeDtypeStruct((devices * ROWS_IN, span), BF16),
        in_specs=[pl.BlockSpec(memory_space=pltpu.HBM)] * 2,
        out_specs=pl.BlockSpec(memory_space=pltpu.HBM),
        scratch_shapes=[
            pltpu.VMEM((2, span, channels), BF16),
            pltpu.VMEM((devices * ROWS_IN, span), F32),
            pltpu.VMEM((devices * ROWS_IN, span), BF16),
            pltpu.SemaphoreType.DMA((2 + SEND_PIECES,)),
        ],
    )(inputs[0], grad_out[0])
    recv = lax.all_to_all(
        sent.reshape(devices, ROWS_IN, span), OWNER, split_axis=0, concat_axis=0, tiled=True
    ).reshape(devices * ROWS_IN, span)

    def own(value):
        turned = value.T
        pair = [
            lax.dynamic_slice_in_dim(turned, place + k * devices, 1, axis=1) for k in range(2)
        ]
        return jnp.concatenate(pair, axis=0)[:, 0]

    def own_flat(value):
        pair = [lax.dynamic_slice_in_dim(value, place + k * devices, 1) for k in range(2)]
        return jnp.repeat(jnp.concatenate(pair), poles)

    step_size = jnp.exp(own_flat(log_dt))
    pole_re = -jnp.exp(own(log_a_re))
    im = own(a_im)
    terms = pole_lines(step_size, pole_re, im, own(c_re), own(c_im))
    w_re, w_im, ct_re, ct_im = terms[:4]
    far = jnp.exp(w_re * span)
    gains = [
        jnp.broadcast_to(lax.dynamic_slice_in_dim(skip_gain, place + k * devices, 1), (span,))
        for k in range(2)
    ]
    prm = jnp.stack(
        [far * jnp.cos(w_im * span), far * jnp.sin(w_im * span)]
        + list(terms[2:])
        + [step_size, pole_re, w_re, w_im]
        + gains
    )
    cols = jnp.stack([w_re, w_im, ct_re, ct_im], axis=1)
    wide = 2 * span
    tall = jax.ShapeDtypeStruct((4 * 2 * poles, wide), BF16)
    square = jax.ShapeDtypeStruct((wide, wide), BF16)
    tables = pl.pallas_call(
        table_kernel,
        out_shape=[tall] * 4 + [square] * 5,
        in_specs=vmem(1),
        out_specs=vmem(9),
        compiler_params=LIMIT,
    )(cols)
    grid = pltpu.VMEM((devices, span), F32)
    answer = pl.pallas_call(
        functools.partial(core_kernel, batch),
        out_shape=jax.ShapeDtypeStruct((chips * ROWS_OUT, span), BF16),
        in_specs=vmem(11),
        out_specs=vmem(1)[0],
        scratch_shapes=[pltpu.VMEM((devices * ROWS_IN, span), F32)]
        + [grid] * 10
        + [pltpu.VMEM((2, devices, span), F32)]
        + [pltpu.VMEM((chips * ROWS_OUT, span), F32)],
        compiler_params=LIMIT,
    )(recv, *tables, prm)
    mine = lax.all_to_all(
        answer.reshape(chips, ROWS_OUT // 2, 2, span), CHIP, split_axis=0, concat_axis=0, tiled=True
    ).reshape(chips * ROWS_OUT, span)
    other = lax.ppermute(mine, "core", [(0, 1), (1, 0)])
    line = jax.ShapeDtypeStruct((poles, channels), F32)
    single = jax.ShapeDtypeStruct((1, channels), F32)
    results = pl.pallas_call(
        finish_kernel,
        out_shape=[jax.ShapeDtypeStruct((span, channels), BF16)] + [line] * 4 + [single] * 2,
        in_specs=[pl.BlockSpec(memory_space=pltpu.SMEM)] + vmem(2),
        out_specs=vmem(7),
        scratch_shapes=[pltpu.VMEM((2, chips * ROWS_OUT, span), F32)],
        compiler_params=LIMIT,
    )(lax.axis_index("core").reshape(1), mine, other)
    return (
        results[0][None],
        results[5].reshape(channels),
        results[1].T,
        results[2].T,
        results[3].T,
        results[4].T,
        results[6].reshape(channels),
    )


def solution(mesh):
    pairs, ctx = mesh.devices.shape[0] // 2, mesh.devices.shape[1]
    fine = Mesh(mesh.devices.reshape(pairs, 2, ctx), ("dpair", "core", "ctx"))
    block = P(("dpair", "core"), "ctx", None)
    return jax.shard_map(
        body,
        mesh=fine,
        in_specs=(block, block, P(), P(), P(), P(), P(), P()),
        out_specs=(block, P(), P(), P(), P(), P(), P()),
        check_vma=False,
    )
```

```python
import functools

import jax
import jax.numpy as jnp
from jax import lax
from jax.experimental import pallas as pl
from jax.experimental.pallas import tpu as pltpu
from jax.sharding import Mesh
from jax.sharding import PartitionSpec as P

OWNER = ("ctx", "dpair", "core")
CHIP = ("ctx", "dpair")
F32 = jnp.float32
BF16 = jnp.bfloat16
ROWS_IN = 4
ROWS_OUT = 10
SEND_PIECES = 4
SPARE = 8
LIMIT = pltpu.CompilerParams(vmem_limit_bytes=16 * 1024 * 1024)
FLIP = (((1,), (1,)), ((), ()))
PLAIN = (((1,), (0,)), ((), ()))
OUTER = (((0,), (0,)), ((), ()))


def halves(value):
    high = value.astype(BF16)
    low = (value - high.astype(F32)).astype(BF16)
    return (high, low)


def dot(a, b, dims):
    return lax.dot_general(a, b, dims, preferred_element_type=F32)


def send_kernel(inputs_ref, grad_ref, out_ref, stage, rows, packed, sems):
    owners = packed.shape[0] // ROWS_IN
    chips = owners // 2
    loads = [
        pltpu.make_async_copy(ref, stage.at[part], sems.at[part])
        for part, ref in enumerate((inputs_ref, grad_ref))
    ]
    for load in loads:
        load.start()
    for part, load in enumerate(loads):
        load.wait()
        for half in range(2):
            for core in range(2):
                at = half * owners + core * chips
                piece = stage[part, :, at : at + chips].astype(F32).T
                line = ROWS_IN * core + 2 * part + half
                rows[pl.ds(line, chips, stride=2 * ROWS_IN), :] = piece
    pieces = sems.shape[0] - 2
    size = packed.shape[0] // pieces
    stores = []
    for index in range(pieces):
        at = pl.ds(index * size, size)
        packed[at, :] = rows[at, :].astype(BF16)
        stores.append(pltpu.make_async_copy(packed.at[at, :], out_ref.at[at, :], sems.at[2 + index]))
        stores[-1].start()
    for store in stores:
        store.wait()


def table_kernel(cols_ref, fwd_hi, fwd_lo, rev_hi, rev_lo, mix_hi, mix_lo, band_hi, band_lo, flip_ref):
    poles = cols_ref.shape[0]
    half = poles // 2
    span = poles
    w_re, w_im = cols_ref[:, 0:1], cols_ref[:, 1:2]
    ct_re, ct_im = cols_ref[:, 2:3], cols_ref[:, 3:4]
    lane = lax.broadcasted_iota(jnp.int32, (poles, span), 1)
    sub = lax.broadcasted_iota(jnp.int32, (poles, span), 0)
    first = sub < half

    def spread(value):
        return jnp.concatenate([jnp.where(first, value, 0.0), jnp.where(first, 0.0, value)], axis=1)

    def put(hi_ref, lo_ref, part, value):
        hi, lo = halves(spread(value))
        hi_ref[part * poles : (part + 1) * poles, :] = hi
        lo_ref[part * poles : (part + 1) * poles, :] = lo

    step = lane.astype(F32)
    grow = jnp.exp(w_re * step)
    turn = w_im * step
    f_re, f_im = grow * jnp.cos(turn), grow * jnp.sin(turn)
    put(fwd_hi, fwd_lo, 0, f_re)
    put(fwd_hi, fwd_lo, 1, f_im)
    put(fwd_hi, fwd_lo, 2, f_re * step)
    put(fwd_hi, fwd_lo, 3, f_im * step)
    back = (span - lane).astype(F32)
    shrink = jnp.exp(w_re * back)
    twist = w_im * back
    h_re, h_im = shrink * jnp.cos(twist), shrink * jnp.sin(twist)
    put(rev_hi, rev_lo, 0, h_re)
    put(rev_hi, rev_lo, 1, h_im)
    put(rev_hi, rev_lo, 2, h_re * back)
    put(rev_hi, rev_lo, 3, h_im * back)
    put(mix_hi, mix_lo, 0, 2.0 * (ct_re * h_re - ct_im * h_im))
    put(mix_hi, mix_lo, 1, -2.0 * (ct_re * h_im + ct_im * h_re))
    taps = 2.0 * (ct_re * f_re - ct_im * f_im)
    upper = lane >= sub
    zero = jnp.zeros((span, span), F32)
    for chan in range(2):
        line = jnp.sum(taps[chan * half : (chan + 1) * half, :], axis=0, keepdims=True)
        band = pltpu.roll(jnp.broadcast_to(line, (span, span)), 0, 1, stride=1, stride_axis=0)
        band = jnp.where(upper, band, 0.0)
        wide = jnp.concatenate([band, zero] if chan == 0 else [zero, band], axis=1)
        hi, lo = halves(wide)
        band_hi[chan * span : (chan + 1) * span, :] = hi
        band_lo[chan * span : (chan + 1) * span, :] = lo
    wide_sub = lax.broadcasted_iota(jnp.int32, flip_ref.shape, 0)
    wide_lane = lax.broadcasted_iota(jnp.int32, flip_ref.shape, 1)
    same = (wide_sub < span) == (wide_lane < span)
    mirror = (wide_sub % span) + (wide_lane % span) == span - 1
    flip_ref[...] = jnp.where(same & mirror, 1.0, 0.0).astype(BF16)


def diagonals(value):
    sub = lax.broadcasted_iota(jnp.int32, value.shape, 0)
    lane = lax.broadcasted_iota(jnp.int32, value.shape, 1)
    value = jnp.where(lane + sub >= value.shape[0] - 1, value, 0.0)
    return pltpu.roll(value, 1, 1, stride=1, stride_axis=0)


def core_kernel(
    batch,
    recv_ref,
    fwd_hi,
    fwd_lo,
    rev_hi,
    rev_lo,
    mix_hi,
    mix_lo,
    band_hi,
    band_lo,
    flip_ref,
    prm_ref,
    out_ref,
    rows,
    g_re,
    g_im,
    d_re,
    d_im,
    z_re,
    z_im,
    v_re,
    v_im,
    x_re,
    x_im,
    base,
    outs,
):
    sources = recv_ref.shape[0] // ROWS_IN
    chunks = sources // batch
    poles = prm_ref.shape[1]
    span = poles
    half = poles // 2
    rows[: sources * ROWS_IN, :] = recv_ref[...].astype(F32)

    def part(index):
        return rows[pl.ds(index, sources, stride=ROWS_IN), :]

    u_f = jnp.concatenate([part(0), part(1)], axis=1)
    g_f = jnp.concatenate([part(2), part(3)], axis=1)
    u_b, g_b = u_f.astype(BF16), g_f.astype(BF16)
    prm = prm_ref[...]

    def line(index):
        return prm[index : index + 1, :]

    def total(value):
        return jnp.sum(value, axis=0, keepdims=True)

    mirrored = dot(flip_ref[...], u_b, FLIP).astype(BF16)
    cross = dot(mirrored, g_b, PLAIN)
    lead = dot(u_b, rev_hi[...], FLIP) + dot(u_b, rev_lo[...], FLIP)
    for index, ref in enumerate((v_re, v_im, x_re, x_im)):
        ref[:sources, :] = lead[:, index * poles : (index + 1) * poles]
    near_back = dot(g_b, band_hi[...], FLIP) + dot(g_b, band_lo[...], FLIP)
    near_back = near_back + jnp.concatenate([line(14), line(15)], axis=1) * g_f
    blocks = [cross[k * span : (k + 1) * span, k * span : (k + 1) * span] for k in range(2)]
    lag = jnp.concatenate([total(diagonals(value)) for value in blocks], axis=1)
    lag_hi, lag_lo = halves(jnp.broadcast_to(lag, (16, 2 * span)))
    stacked = jnp.concatenate([g_b, lag_hi, lag_lo], axis=0)
    moments = dot(stacked, fwd_hi[...], FLIP) + dot(stacked, fwd_lo[...], FLIP)
    near = moments[sources : sources + 1] + moments[sources + 16 : sources + 17]
    moments = moments[:sources]
    for index, ref in enumerate((g_re, g_im, d_re, d_im)):
        ref[:sources, :] = moments[:, index * poles : (index + 1) * poles]
    e_re, e_im = line(0), line(1)
    a, b, c, d, s_re, s_im, t_re, t_im = (jnp.zeros((batch, poles), F32) for _ in range(8))
    for chunk in reversed(range(chunks)):
        at = pl.ds(chunk * batch, batch)
        z_re[at, :] = a
        z_im[at, :] = b
        if chunk < chunks - 1:
            p, q, x, y = v_re[at, :], v_im[at, :], x_re[at, :], x_im[at, :]
            s_re, s_im = s_re + (p * a - q * b), s_im + (p * b + q * a)
            t_re = t_re + (x * a - y * b) + (p * c - q * d)
            t_im = t_im + (x * b + y * a) + (p * d + q * c)
        if chunk > 0:
            m = c + span * a
            n = d + span * b
            a, b = (e_re * a - e_im * b) + g_re[at, :], (e_re * b + e_im * a) + g_im[at, :]
            c, d = (e_re * m - e_im * n) + d_re[at, :], (e_re * n + e_im * m) + d_im[at, :]
    s_re, s_im, t_re, t_im = total(s_re), total(s_im), total(t_re), total(t_im)

    state = jnp.concatenate([z_re[:sources, :], z_im[:sources, :]], axis=1)
    state_hi, state_lo = halves(state)
    back = dot(state_hi, mix_hi[...], PLAIN) + dot(state_lo, mix_hi[...], PLAIN)
    back = back + dot(state_hi, mix_lo[...], PLAIN)
    back = back + near_back
    for chan in range(2):
        base[chan, :sources, :] = back[:, chan * span : (chan + 1) * span]

    s_re = s_re + near[:, :poles]
    s_im = s_im + near[:, poles : 2 * poles]
    t_re = t_re + near[:, 2 * poles : 3 * poles]
    t_im = t_im + near[:, 3 * poles :]

    def times(p, q):
        return (p[0] * q[0] - p[1] * q[1], p[0] * q[1] + p[1] * q[0])

    s, t = (s_re, s_im), (t_re, t_im)
    ct, lift = (line(2), line(3)), (line(4), line(5))
    slope, ratio = (line(6), line(7)), (line(8), line(9))
    size, pole_re, w = line(10), line(11), (line(12), line(13))
    by_c = times(s, lift)
    first, second = times(s, slope), times(t, ct)
    by_w = (first[0] + second[0], first[1] + second[1])
    third = times(s, ratio)
    by_a = (size * by_w[0] - third[0], size * by_w[1] - third[1])
    by_dt = 2.0 * (by_w[0] * w[0] - by_w[1] * w[1])
    lane = lax.broadcasted_iota(jnp.int32, (1, poles), 1)
    by_skip = total(u_f * g_f)
    loose = [
        jnp.sum(jnp.where(lane < half, by_dt, 0.0), axis=1, keepdims=True),
        jnp.sum(jnp.where(lane < half, 0.0, by_dt), axis=1, keepdims=True),
        jnp.sum(by_skip[:, :span], axis=1, keepdims=True),
        jnp.sum(by_skip[:, span:], axis=1, keepdims=True),
    ]
    misc = jnp.zeros((1, poles), F32)
    for index, value in enumerate(loose):
        misc = jnp.where(lane == index, value, misc)
    lines = [
        2.0 * by_a[0] * pole_re,
        -2.0 * by_a[1],
        2.0 * by_c[0],
        -2.0 * by_c[1],
        misc,
        jnp.zeros((1, poles), F32),
    ]
    chips = sources // 2
    for core in range(2):
        for chan in range(2):
            outs[pl.ds(2 * core + chan, chips, stride=ROWS_OUT), :] = base[
                chan, pl.ds(core, chips, stride=2), :
            ]
    for index, value in enumerate(lines):
        outs[pl.ds(4 + index, chips, stride=ROWS_OUT), :] = jnp.broadcast_to(value, (chips, poles))
    out_ref[...] = outs[: chips * ROWS_OUT, :].astype(BF16)


def finish_kernel(core_ref, mine_ref, other_ref, grad_ref, a_ref, b_ref, c_ref, d_ref, dt_ref, skip_ref, rows):
    used = mine_ref.shape[0]
    chips = used // ROWS_OUT
    half = a_ref.shape[0]
    core = core_ref[0]
    rows[core, :used, :] = mine_ref[...].astype(F32)
    rows[1 - core, :used, :] = other_ref[...].astype(F32)

    def turned(owner, index):
        return rows[owner, pl.ds(index, chips, stride=ROWS_OUT), :].T

    for owner in range(2):
        for chan in range(2):
            at = (2 * chan + owner) * chips
            grad_ref[:, at : at + chips] = turned(owner, 2 * core + chan).astype(BF16)
        for index, ref in enumerate((a_ref, b_ref, c_ref, d_ref)):
            block = turned(owner, 4 + index)
            for chan in range(2):
                at = (2 * chan + owner) * chips
                ref[:, at : at + chips] = block[chan * half : (chan + 1) * half]
        misc = turned(owner, 8)
        for chan in range(2):
            at = (2 * chan + owner) * chips
            dt_ref[:, at : at + chips] = misc[chan : chan + 1]
            skip_ref[:, at : at + chips] = misc[2 + chan : 3 + chan]


def pole_lines(step_size, pole_re, a_im, c_re, c_im):
    w_re = step_size * pole_re
    w_im = step_size * a_im
    growth = jnp.exp(w_re)
    cosine, sine = jnp.cos(w_im), jnp.sin(w_im)
    half_sin = jnp.sin(0.5 * w_im)
    e_re = jnp.expm1(w_re) * cosine - 2.0 * half_sin * half_sin
    e_im = growth * sine
    modulus = pole_re * pole_re + a_im * a_im

    def over_pole(re, im):
        return ((re * pole_re + im * a_im) / modulus, (im * pole_re - re * a_im) / modulus)

    ct_re, ct_im = over_pole(e_re * c_re - e_im * c_im, e_re * c_im + e_im * c_re)
    lift = over_pole(e_re, e_im)
    g_re, g_im = growth * cosine, growth * sine
    slope = over_pole(g_re * c_re - g_im * c_im, g_re * c_im + g_im * c_re)
    ratio = over_pole(ct_re, ct_im)
    return (w_re, w_im, ct_re, ct_im) + lift + slope + ratio


def vmem(count):
    return [pl.BlockSpec(memory_space=pltpu.VMEM)] * count


def body(inputs, grad_out, log_dt, log_a_re, a_im, c_re, c_im, skip_gain):
    batch = lax.axis_size("dpair") * lax.axis_size("core")
    devices = batch * lax.axis_size("ctx")
    span, channels = inputs.shape[1:]
    poles = a_im.shape[1]
    assert channels == 2 * devices and span == 2 * poles
    chips = devices // 2
    place = lax.axis_index("core") * chips + lax.axis_index(CHIP)

    sent = pl.pallas_call(
        send_kernel,
        out_shape=jax.ShapeDtypeStruct((devices * ROWS_IN, span), BF16),
        in_specs=[pl.BlockSpec(memory_space=pltpu.HBM)] * 2,
        out_specs=pl.BlockSpec(memory_space=pltpu.HBM),
        scratch_shapes=[
            pltpu.VMEM((2, span, channels), BF16),
            pltpu.VMEM(((devices + 2 * SPARE) * ROWS_IN, span), F32),
            pltpu.VMEM((devices * ROWS_IN, span), BF16),
            pltpu.SemaphoreType.DMA((2 + SEND_PIECES,)),
        ],
    )(inputs[0], grad_out[0])
    recv = lax.all_to_all(
        sent.reshape(devices, ROWS_IN, span), OWNER, split_axis=0, concat_axis=0, tiled=True
    ).reshape(devices * ROWS_IN, span)

    def own(value):
        turned = value.T
        pair = [
            lax.dynamic_slice_in_dim(turned, place + k * devices, 1, axis=1) for k in range(2)
        ]
        return jnp.concatenate(pair, axis=0)[:, 0]

    def own_flat(value):
        pair = [lax.dynamic_slice_in_dim(value, place + k * devices, 1) for k in range(2)]
        return jnp.repeat(jnp.concatenate(pair), poles)

    step_size = jnp.exp(own_flat(log_dt))
    pole_re = -jnp.exp(own(log_a_re))
    im = own(a_im)
    terms = pole_lines(step_size, pole_re, im, own(c_re), own(c_im))
    w_re, w_im, ct_re, ct_im = terms[:4]
    far = jnp.exp(w_re * span)
    gains = [
        jnp.broadcast_to(lax.dynamic_slice_in_dim(skip_gain, place + k * devices, 1), (span,))
        for k in range(2)
    ]
    prm = jnp.stack(
        [far * jnp.cos(w_im * span), far * jnp.sin(w_im * span)]
        + list(terms[2:])
        + [step_size, pole_re, w_re, w_im]
        + gains
    )
    cols = jnp.stack([w_re, w_im, ct_re, ct_im], axis=1)
    wide = 2 * span
    tall = jax.ShapeDtypeStruct((4 * 2 * poles, wide), BF16)
    square = jax.ShapeDtypeStruct((wide, wide), BF16)
    tables = pl.pallas_call(
        table_kernel,
        out_shape=[tall] * 4 + [square] * 5,
        in_specs=vmem(1),
        out_specs=vmem(9),
        compiler_params=LIMIT,
    )(cols)
    grid = pltpu.VMEM((devices + SPARE, span), F32)
    answer = pl.pallas_call(
        functools.partial(core_kernel, batch),
        out_shape=jax.ShapeDtypeStruct((chips * ROWS_OUT, span), BF16),
        in_specs=vmem(11),
        out_specs=vmem(1)[0],
        scratch_shapes=[pltpu.VMEM(((devices + SPARE) * ROWS_IN, span), F32)]
        + [grid] * 10
        + [pltpu.VMEM((2, devices + 2 * SPARE, span), F32)]
        + [pltpu.VMEM(((chips + SPARE) * ROWS_OUT, span), F32)],
        compiler_params=LIMIT,
    )(recv, *tables, prm)
    mine = lax.all_to_all(
        answer.reshape(chips, ROWS_OUT // 2, 2, span), CHIP, split_axis=0, concat_axis=0, tiled=True
    ).reshape(chips * ROWS_OUT, span)
    other = lax.ppermute(mine, "core", [(0, 1), (1, 0)])
    line = jax.ShapeDtypeStruct((poles, channels), F32)
    single = jax.ShapeDtypeStruct((1, channels), F32)
    results = pl.pallas_call(
        finish_kernel,
        out_shape=[jax.ShapeDtypeStruct((span, channels), BF16)] + [line] * 4 + [single] * 2,
        in_specs=[pl.BlockSpec(memory_space=pltpu.SMEM)] + vmem(2),
        out_specs=vmem(7),
        scratch_shapes=[pltpu.VMEM((2, (chips + SPARE) * ROWS_OUT, span), F32)],
        compiler_params=LIMIT,
    )(lax.axis_index("core").reshape(1), mine, other)
    return (
        results[0][None],
        results[5].reshape(channels),
        results[1].T,
        results[2].T,
        results[3].T,
        results[4].T,
        results[6].reshape(channels),
    )


def solution(mesh):
    pairs, ctx = mesh.devices.shape[0] // 2, mesh.devices.shape[1]
    fine = Mesh(mesh.devices.reshape(pairs, 2, ctx), ("dpair", "core", "ctx"))
    block = P(("dpair", "core"), "ctx", None)
    return jax.shard_map(
        body,
        mesh=fine,
        in_specs=(block, block, P(), P(), P(), P(), P(), P()),
        out_specs=(block, P(), P(), P(), P(), P(), P()),
        check_vma=False,
    )
```

```python
import functools
import math

import jax
import jax.numpy as jnp
from jax import lax
from jax.experimental import pallas as pl
from jax.experimental.pallas import tpu as pltpu
from jax.sharding import Mesh
from jax.sharding import PartitionSpec as P

OWNER = ("ctx", "dpair", "core")
CHIP = ("ctx", "dpair")
F32 = jnp.float32
BF16 = jnp.bfloat16
ROWS_IN = 4
ROWS_OUT = 10
SEND_PIECES = 4
SPARE = 8
SERIES = [(k - 1) / math.factorial(k) for k in range(2, 12)]
LIMIT = pltpu.CompilerParams(vmem_limit_bytes=16 * 1024 * 1024)
FLIP = (((1,), (1,)), ((), ()))
PLAIN = (((1,), (0,)), ((), ()))
OUTER = (((0,), (0,)), ((), ()))


def halves(value):
    high = value.astype(BF16)
    low = (value - high.astype(F32)).astype(BF16)
    return (high, low)


def times(p, q):
    return (p[0] * q[0] - p[1] * q[1], p[0] * q[1] + p[1] * q[0])


def dot(a, b, dims):
    return lax.dot_general(a, b, dims, preferred_element_type=F32)


def send_kernel(inputs_ref, grad_ref, out_ref, stage, rows, packed, sems):
    owners = packed.shape[0] // ROWS_IN
    chips = owners // 2
    loads = [
        pltpu.make_async_copy(ref, stage.at[part], sems.at[part])
        for part, ref in enumerate((inputs_ref, grad_ref))
    ]
    for load in loads:
        load.start()
    for part, load in enumerate(loads):
        load.wait()
        for half in range(2):
            for core in range(2):
                at = half * owners + core * chips
                piece = stage[part, :, at : at + chips].astype(F32).T
                line = ROWS_IN * core + 2 * part + half
                rows[pl.ds(line, chips, stride=2 * ROWS_IN), :] = piece
    pieces = sems.shape[0] - 2
    size = packed.shape[0] // pieces
    stores = []
    for index in range(pieces):
        at = pl.ds(index * size, size)
        packed[at, :] = rows[at, :].astype(BF16)
        stores.append(pltpu.make_async_copy(packed.at[at, :], out_ref.at[at, :], sems.at[2 + index]))
        stores[-1].start()
    for store in stores:
        store.wait()


def table_kernel(cols_ref, fwd_hi, fwd_lo, rev_hi, rev_lo, mix_hi, mix_lo, band_hi, band_lo, flip_ref):
    poles = cols_ref.shape[0]
    half = poles // 2
    span = poles
    w_re, w_im = cols_ref[:, 0:1], cols_ref[:, 1:2]
    ct_re, ct_im = cols_ref[:, 2:3], cols_ref[:, 3:4]
    lane = lax.broadcasted_iota(jnp.int32, (poles, span), 1)
    sub = lax.broadcasted_iota(jnp.int32, (poles, span), 0)
    first = sub < half

    def spread(value):
        return jnp.concatenate([jnp.where(first, value, 0.0), jnp.where(first, 0.0, value)], axis=1)

    def put(hi_ref, lo_ref, part, value):
        hi, lo = halves(spread(value))
        hi_ref[part * poles : (part + 1) * poles, :] = hi
        lo_ref[part * poles : (part + 1) * poles, :] = lo

    step = lane.astype(F32)
    grow = jnp.exp(w_re * step)
    turn = w_im * step
    f_re, f_im = grow * jnp.cos(turn), grow * jnp.sin(turn)
    put(fwd_hi, fwd_lo, 0, f_re)
    put(fwd_hi, fwd_lo, 1, f_im)
    put(fwd_hi, fwd_lo, 2, f_re * step)
    put(fwd_hi, fwd_lo, 3, f_im * step)
    back = (span - lane).astype(F32)
    shrink = jnp.exp(w_re * back)
    twist = w_im * back
    h_re, h_im = shrink * jnp.cos(twist), shrink * jnp.sin(twist)
    put(rev_hi, rev_lo, 0, h_re)
    put(rev_hi, rev_lo, 1, h_im)
    put(rev_hi, rev_lo, 2, h_re * back)
    put(rev_hi, rev_lo, 3, h_im * back)
    put(mix_hi, mix_lo, 0, 2.0 * (ct_re * h_re - ct_im * h_im))
    put(mix_hi, mix_lo, 1, -2.0 * (ct_re * h_im + ct_im * h_re))
    taps = 2.0 * (ct_re * f_re - ct_im * f_im)
    upper = lane >= sub
    zero = jnp.zeros((span, span), F32)
    for chan in range(2):
        line = jnp.sum(taps[chan * half : (chan + 1) * half, :], axis=0, keepdims=True)
        band = pltpu.roll(jnp.broadcast_to(line, (span, span)), 0, 1, stride=1, stride_axis=0)
        band = jnp.where(upper, band, 0.0)
        wide = jnp.concatenate([band, zero] if chan == 0 else [zero, band], axis=1)
        hi, lo = halves(wide)
        band_hi[chan * span : (chan + 1) * span, :] = hi
        band_lo[chan * span : (chan + 1) * span, :] = lo
    wide_sub = lax.broadcasted_iota(jnp.int32, flip_ref.shape, 0)
    wide_lane = lax.broadcasted_iota(jnp.int32, flip_ref.shape, 1)
    same = (wide_sub < span) == (wide_lane < span)
    mirror = (wide_sub % span) + (wide_lane % span) == span - 1
    flip_ref[...] = jnp.where(same & mirror, 1.0, 0.0).astype(BF16)


def diagonals(value):
    sub = lax.broadcasted_iota(jnp.int32, value.shape, 0)
    lane = lax.broadcasted_iota(jnp.int32, value.shape, 1)
    value = jnp.where(lane + sub >= value.shape[0] - 1, value, 0.0)
    return pltpu.roll(value, 1, 1, stride=1, stride_axis=0)


def core_kernel(
    batch,
    recv_ref,
    fwd_hi,
    fwd_lo,
    rev_hi,
    rev_lo,
    mix_hi,
    mix_lo,
    band_hi,
    band_lo,
    flip_ref,
    prm_ref,
    out_ref,
    rows,
    g_re,
    g_im,
    d_re,
    d_im,
    z_re,
    z_im,
    v_re,
    v_im,
    x_re,
    x_im,
    base,
    outs,
):
    sources = recv_ref.shape[0] // ROWS_IN
    chunks = sources // batch
    poles = prm_ref.shape[1]
    span = poles
    half = poles // 2
    rows[: sources * ROWS_IN, :] = recv_ref[...].astype(F32)

    def part(index):
        return rows[pl.ds(index, sources, stride=ROWS_IN), :]

    u_f = jnp.concatenate([part(0), part(1)], axis=1)
    g_f = jnp.concatenate([part(2), part(3)], axis=1)
    u_b, g_b = u_f.astype(BF16), g_f.astype(BF16)
    prm = prm_ref[...]

    def line(index):
        return prm[index : index + 1, :]

    def total(value):
        return jnp.sum(value, axis=0, keepdims=True)

    mirrored = dot(flip_ref[...], u_b, FLIP).astype(BF16)
    cross = dot(mirrored, g_b, PLAIN)
    lead = dot(u_b, rev_hi[...], FLIP) + dot(u_b, rev_lo[...], FLIP)
    for index, ref in enumerate((v_re, v_im, x_re, x_im)):
        ref[:sources, :] = lead[:, index * poles : (index + 1) * poles]
    near_back = dot(g_b, band_hi[...], FLIP) + dot(g_b, band_lo[...], FLIP)
    near_back = near_back + jnp.concatenate([line(14), line(15)], axis=1) * g_f
    blocks = [cross[k * span : (k + 1) * span, k * span : (k + 1) * span] for k in range(2)]
    lag = jnp.concatenate([total(diagonals(value)) for value in blocks], axis=1)
    lag_hi, lag_lo = halves(jnp.broadcast_to(lag, (16, 2 * span)))
    stacked = jnp.concatenate([g_b, lag_hi, lag_lo], axis=0)
    moments = dot(stacked, fwd_hi[...], FLIP) + dot(stacked, fwd_lo[...], FLIP)
    near = moments[sources : sources + 1] + moments[sources + 16 : sources + 17]
    moments = moments[:sources]
    for index, ref in enumerate((g_re, g_im, d_re, d_im)):
        ref[:sources, :] = moments[:, index * poles : (index + 1) * poles]
    e_re, e_im = line(0), line(1)
    a, b, c, d, s_re, s_im, t_re, t_im = (jnp.zeros((batch, poles), F32) for _ in range(8))
    for chunk in reversed(range(chunks)):
        at = pl.ds(chunk * batch, batch)
        z_re[at, :] = a
        z_im[at, :] = b
        if chunk < chunks - 1:
            p, q, x, y = v_re[at, :], v_im[at, :], x_re[at, :], x_im[at, :]
            s_re, s_im = s_re + (p * a - q * b), s_im + (p * b + q * a)
            t_re = t_re + (x * a - y * b) + (p * c - q * d)
            t_im = t_im + (x * b + y * a) + (p * d + q * c)
        if chunk > 0:
            m = c + span * a
            n = d + span * b
            a, b = (e_re * a - e_im * b) + g_re[at, :], (e_re * b + e_im * a) + g_im[at, :]
            c, d = (e_re * m - e_im * n) + d_re[at, :], (e_re * n + e_im * m) + d_im[at, :]
    s_re, s_im, t_re, t_im = total(s_re), total(s_im), total(t_re), total(t_im)

    state = jnp.concatenate([z_re[:sources, :], z_im[:sources, :]], axis=1)
    state_hi, state_lo = halves(state)
    back = dot(state_hi, mix_hi[...], PLAIN) + dot(state_lo, mix_hi[...], PLAIN)
    back = back + dot(state_hi, mix_lo[...], PLAIN)
    back = back + near_back
    for chan in range(2):
        base[chan, :sources, :] = back[:, chan * span : (chan + 1) * span]

    s_re = s_re + near[:, :poles]
    s_im = s_im + near[:, poles : 2 * poles]
    t_re = t_re + near[:, 2 * poles : 3 * poles]
    t_im = t_im + near[:, 3 * poles :]

    s, t = (s_re, s_im), (t_re, t_im)
    ct, lift = (line(2), line(3)), (line(4), line(5))
    slope, curve = (line(6), line(7)), (line(8), line(9))
    size, pole_re, w = line(10), line(11), (line(12), line(13))
    by_c = times(s, lift)
    first, second = times(s, slope), times(t, ct)
    by_w = (first[0] + second[0], first[1] + second[1])
    third = times(s, curve)
    by_a = (size * second[0] + third[0], size * second[1] + third[1])
    by_dt = 2.0 * (by_w[0] * w[0] - by_w[1] * w[1])
    lane = lax.broadcasted_iota(jnp.int32, (1, poles), 1)
    by_skip = total(u_f * g_f)
    loose = [
        jnp.sum(jnp.where(lane < half, by_dt, 0.0), axis=1, keepdims=True),
        jnp.sum(jnp.where(lane < half, 0.0, by_dt), axis=1, keepdims=True),
        jnp.sum(by_skip[:, :span], axis=1, keepdims=True),
        jnp.sum(by_skip[:, span:], axis=1, keepdims=True),
    ]
    misc = jnp.zeros((1, poles), F32)
    for index, value in enumerate(loose):
        misc = jnp.where(lane == index, value, misc)
    lines = [
        2.0 * by_a[0] * pole_re,
        -2.0 * by_a[1],
        2.0 * by_c[0],
        -2.0 * by_c[1],
        misc,
        jnp.zeros((1, poles), F32),
    ]
    chips = sources // 2
    for core in range(2):
        for chan in range(2):
            outs[pl.ds(2 * core + chan, chips, stride=ROWS_OUT), :] = base[
                chan, pl.ds(core, chips, stride=2), :
            ]
    for index, value in enumerate(lines):
        outs[pl.ds(4 + index, chips, stride=ROWS_OUT), :] = jnp.broadcast_to(value, (chips, poles))
    out_ref[...] = outs[: chips * ROWS_OUT, :].astype(BF16)


def finish_kernel(core_ref, mine_ref, other_ref, grad_ref, a_ref, b_ref, c_ref, d_ref, dt_ref, skip_ref, rows):
    used = mine_ref.shape[0]
    chips = used // ROWS_OUT
    half = a_ref.shape[0]
    core = core_ref[0]
    rows[core, :used, :] = mine_ref[...].astype(F32)
    rows[1 - core, :used, :] = other_ref[...].astype(F32)

    def turned(owner, index):
        return rows[owner, pl.ds(index, chips, stride=ROWS_OUT), :].T

    for owner in range(2):
        for chan in range(2):
            at = (2 * chan + owner) * chips
            grad_ref[:, at : at + chips] = turned(owner, 2 * core + chan).astype(BF16)
        for index, ref in enumerate((a_ref, b_ref, c_ref, d_ref)):
            block = turned(owner, 4 + index)
            for chan in range(2):
                at = (2 * chan + owner) * chips
                ref[:, at : at + chips] = block[chan * half : (chan + 1) * half]
        misc = turned(owner, 8)
        for chan in range(2):
            at = (2 * chan + owner) * chips
            dt_ref[:, at : at + chips] = misc[chan : chan + 1]
            skip_ref[:, at : at + chips] = misc[2 + chan : 3 + chan]


def lifted(w, growth, rise):
    tail = (jnp.full_like(w[0], SERIES[-1]), jnp.zeros_like(w[0]))
    for value in reversed(SERIES[:-1]):
        tail = times(tail, w)
        tail = (tail[0] + value, tail[1])
    near = times(times(w, w), tail)
    far = times(w, growth)
    small = w[0] * w[0] + w[1] * w[1] < 0.25
    return tuple(jnp.where(small, near[k], far[k] - rise[k]) for k in range(2))


def pole_lines(step_size, pole_re, a_im, c_re, c_im):
    w = (step_size * pole_re, step_size * a_im)
    growth = jnp.exp(w[0])
    cosine, sine = jnp.cos(w[1]), jnp.sin(w[1])
    half_sin = jnp.sin(0.5 * w[1])
    rise = (jnp.expm1(w[0]) * cosine - 2.0 * half_sin * half_sin, growth * sine)
    growth = (growth * cosine, growth * sine)
    modulus = pole_re * pole_re + a_im * a_im
    inverse = (pole_re / modulus, -a_im / modulus)
    c = (c_re, c_im)
    lift = times(rise, inverse)
    slope = times(times(growth, c), inverse)
    curve = times(times(times(lifted(w, growth, rise), inverse), inverse), c)
    return w + times(lift, c) + lift + slope + curve


def vmem(count):
    return [pl.BlockSpec(memory_space=pltpu.VMEM)] * count


def body(inputs, grad_out, log_dt, log_a_re, a_im, c_re, c_im, skip_gain):
    batch = lax.axis_size("dpair") * lax.axis_size("core")
    devices = batch * lax.axis_size("ctx")
    span, channels = inputs.shape[1:]
    poles = a_im.shape[1]
    assert channels == 2 * devices and span == 2 * poles
    chips = devices // 2
    place = lax.axis_index("core") * chips + lax.axis_index(CHIP)

    sent = pl.pallas_call(
        send_kernel,
        out_shape=jax.ShapeDtypeStruct((devices * ROWS_IN, span), BF16),
        in_specs=[pl.BlockSpec(memory_space=pltpu.HBM)] * 2,
        out_specs=pl.BlockSpec(memory_space=pltpu.HBM),
        scratch_shapes=[
            pltpu.VMEM((2, span, channels), BF16),
            pltpu.VMEM(((devices + 2 * SPARE) * ROWS_IN, span), F32),
            pltpu.VMEM((devices * ROWS_IN, span), BF16),
            pltpu.SemaphoreType.DMA((2 + SEND_PIECES,)),
        ],
    )(inputs[0], grad_out[0])
    recv = lax.all_to_all(
        sent.reshape(devices, ROWS_IN, span), OWNER, split_axis=0, concat_axis=0, tiled=True
    ).reshape(devices * ROWS_IN, span)

    def own(value):
        turned = value.T
        pair = [
            lax.dynamic_slice_in_dim(turned, place + k * devices, 1, axis=1) for k in range(2)
        ]
        return jnp.concatenate(pair, axis=0)[:, 0]

    def own_flat(value):
        pair = [lax.dynamic_slice_in_dim(value, place + k * devices, 1) for k in range(2)]
        return jnp.repeat(jnp.concatenate(pair), poles)

    step_size = jnp.exp(own_flat(log_dt))
    pole_re = -jnp.exp(own(log_a_re))
    im = own(a_im)
    terms = pole_lines(step_size, pole_re, im, own(c_re), own(c_im))
    w_re, w_im, ct_re, ct_im = terms[:4]
    far = jnp.exp(w_re * span)
    gains = [
        jnp.broadcast_to(lax.dynamic_slice_in_dim(skip_gain, place + k * devices, 1), (span,))
        for k in range(2)
    ]
    prm = jnp.stack(
        [far * jnp.cos(w_im * span), far * jnp.sin(w_im * span)]
        + list(terms[2:])
        + [step_size, pole_re, w_re, w_im]
        + gains
    )
    cols = jnp.stack([w_re, w_im, ct_re, ct_im], axis=1)
    wide = 2 * span
    tall = jax.ShapeDtypeStruct((4 * 2 * poles, wide), BF16)
    square = jax.ShapeDtypeStruct((wide, wide), BF16)
    tables = pl.pallas_call(
        table_kernel,
        out_shape=[tall] * 4 + [square] * 5,
        in_specs=vmem(1),
        out_specs=vmem(9),
        compiler_params=LIMIT,
    )(cols)
    grid = pltpu.VMEM((devices + SPARE, span), F32)
    answer = pl.pallas_call(
        functools.partial(core_kernel, batch),
        out_shape=jax.ShapeDtypeStruct((chips * ROWS_OUT, span), BF16),
        in_specs=vmem(11),
        out_specs=vmem(1)[0],
        scratch_shapes=[pltpu.VMEM(((devices + SPARE) * ROWS_IN, span), F32)]
        + [grid] * 10
        + [pltpu.VMEM((2, devices + 2 * SPARE, span), F32)]
        + [pltpu.VMEM(((chips + SPARE) * ROWS_OUT, span), F32)],
        compiler_params=LIMIT,
    )(recv, *tables, prm)
    mine = lax.all_to_all(
        answer.reshape(chips, ROWS_OUT // 2, 2, span), CHIP, split_axis=0, concat_axis=0, tiled=True
    ).reshape(chips * ROWS_OUT, span)
    other = lax.ppermute(mine, "core", [(0, 1), (1, 0)])
    line = jax.ShapeDtypeStruct((poles, channels), F32)
    single = jax.ShapeDtypeStruct((1, channels), F32)
    results = pl.pallas_call(
        finish_kernel,
        out_shape=[jax.ShapeDtypeStruct((span, channels), BF16)] + [line] * 4 + [single] * 2,
        in_specs=[pl.BlockSpec(memory_space=pltpu.SMEM)] + vmem(2),
        out_specs=vmem(7),
        scratch_shapes=[pltpu.VMEM((2, (chips + SPARE) * ROWS_OUT, span), F32)],
        compiler_params=LIMIT,
    )(lax.axis_index("core").reshape(1), mine, other)
    return (
        results[0][None],
        results[5].reshape(channels),
        results[1].T,
        results[2].T,
        results[3].T,
        results[4].T,
        results[6].reshape(channels),
    )


def solution(mesh):
    pairs, ctx = mesh.devices.shape[0] // 2, mesh.devices.shape[1]
    fine = Mesh(mesh.devices.reshape(pairs, 2, ctx), ("dpair", "core", "ctx"))
    block = P(("dpair", "core"), "ctx", None)
    return jax.shard_map(
        body,
        mesh=fine,
        in_specs=(block, block, P(), P(), P(), P(), P(), P()),
        out_specs=(block, P(), P(), P(), P(), P(), P()),
        check_vma=False,
    )
```

```python
import functools
import math

import jax
import jax.numpy as jnp
from jax import lax
from jax.experimental import pallas as pl
from jax.experimental.pallas import tpu as pltpu
from jax.sharding import Mesh
from jax.sharding import PartitionSpec as P

OWNER = ("ctx", "dpair", "core")
F32 = jnp.float32
BF16 = jnp.bfloat16
ROWS_IN = 4
ROWS_OUT = 10
SEND_PIECES = 4
SPARE = 8
SERIES = [(k - 1) / math.factorial(k) for k in range(2, 12)]
LIMIT = pltpu.CompilerParams(vmem_limit_bytes=16 * 1024 * 1024)
FLIP = (((1,), (1,)), ((), ()))
PLAIN = (((1,), (0,)), ((), ()))
OUTER = (((0,), (0,)), ((), ()))


def halves(value):
    high = value.astype(BF16)
    low = (value - high.astype(F32)).astype(BF16)
    return (high, low)


def times(p, q):
    return (p[0] * q[0] - p[1] * q[1], p[0] * q[1] + p[1] * q[0])


def dot(a, b, dims):
    return lax.dot_general(a, b, dims, preferred_element_type=F32)


def send_kernel(inputs_ref, grad_ref, out_ref, stage, rows, packed, sems):
    owners = packed.shape[0] // ROWS_IN
    chips = owners // 2
    loads = [
        pltpu.make_async_copy(ref, stage.at[part], sems.at[part])
        for part, ref in enumerate((inputs_ref, grad_ref))
    ]
    for load in loads:
        load.start()
    for part, load in enumerate(loads):
        load.wait()
        for half in range(2):
            for core in range(2):
                at = half * owners + core * chips
                piece = stage[part, :, at : at + chips].astype(F32).T
                for pair in range(2):
                    line = ROWS_IN * (2 * pair + core) + 2 * part + half
                    rows[pl.ds(line, chips // 2, stride=4 * ROWS_IN), :] = piece[
                        pair * chips // 2 : (pair + 1) * chips // 2
                    ]
    pieces = sems.shape[0] - 2
    size = packed.shape[0] // pieces
    stores = []
    for index in range(pieces):
        at = pl.ds(index * size, size)
        packed[at, :] = rows[at, :].astype(BF16)
        stores.append(pltpu.make_async_copy(packed.at[at, :], out_ref.at[at, :], sems.at[2 + index]))
        stores[-1].start()
    for store in stores:
        store.wait()


def table_kernel(cols_ref, fwd_hi, fwd_lo, rev_hi, rev_lo, mix_hi, mix_lo, band_hi, band_lo, flip_ref):
    poles = cols_ref.shape[0]
    half = poles // 2
    span = poles
    w_re, w_im = cols_ref[:, 0:1], cols_ref[:, 1:2]
    ct_re, ct_im = cols_ref[:, 2:3], cols_ref[:, 3:4]
    lane = lax.broadcasted_iota(jnp.int32, (poles, span), 1)
    sub = lax.broadcasted_iota(jnp.int32, (poles, span), 0)
    first = sub < half

    def spread(value):
        return jnp.concatenate([jnp.where(first, value, 0.0), jnp.where(first, 0.0, value)], axis=1)

    def put(hi_ref, lo_ref, part, value):
        hi, lo = halves(spread(value))
        hi_ref[part * poles : (part + 1) * poles, :] = hi
        lo_ref[part * poles : (part + 1) * poles, :] = lo

    step = lane.astype(F32)
    grow = jnp.exp(w_re * step)
    turn = w_im * step
    f_re, f_im = grow * jnp.cos(turn), grow * jnp.sin(turn)
    put(fwd_hi, fwd_lo, 0, f_re)
    put(fwd_hi, fwd_lo, 1, f_im)
    put(fwd_hi, fwd_lo, 2, f_re * step)
    put(fwd_hi, fwd_lo, 3, f_im * step)
    back = (span - lane).astype(F32)
    shrink = jnp.exp(w_re * back)
    twist = w_im * back
    h_re, h_im = shrink * jnp.cos(twist), shrink * jnp.sin(twist)
    put(rev_hi, rev_lo, 0, h_re)
    put(rev_hi, rev_lo, 1, h_im)
    put(rev_hi, rev_lo, 2, h_re * back)
    put(rev_hi, rev_lo, 3, h_im * back)
    put(mix_hi, mix_lo, 0, 2.0 * (ct_re * h_re - ct_im * h_im))
    put(mix_hi, mix_lo, 1, -2.0 * (ct_re * h_im + ct_im * h_re))
    taps = 2.0 * (ct_re * f_re - ct_im * f_im)
    upper = lane >= sub
    zero = jnp.zeros((span, span), F32)
    for chan in range(2):
        line = jnp.sum(taps[chan * half : (chan + 1) * half, :], axis=0, keepdims=True)
        band = pltpu.roll(jnp.broadcast_to(line, (span, span)), 0, 1, stride=1, stride_axis=0)
        band = jnp.where(upper, band, 0.0)
        wide = jnp.concatenate([band, zero] if chan == 0 else [zero, band], axis=1)
        hi, lo = halves(wide)
        band_hi[chan * span : (chan + 1) * span, :] = hi
        band_lo[chan * span : (chan + 1) * span, :] = lo
    wide_sub = lax.broadcasted_iota(jnp.int32, flip_ref.shape, 0)
    wide_lane = lax.broadcasted_iota(jnp.int32, flip_ref.shape, 1)
    same = (wide_sub < span) == (wide_lane < span)
    mirror = (wide_sub % span) + (wide_lane % span) == span - 1
    flip_ref[...] = jnp.where(same & mirror, 1.0, 0.0).astype(BF16)


def diagonals(value):
    sub = lax.broadcasted_iota(jnp.int32, value.shape, 0)
    lane = lax.broadcasted_iota(jnp.int32, value.shape, 1)
    value = jnp.where(lane + sub >= value.shape[0] - 1, value, 0.0)
    return pltpu.roll(value, 1, 1, stride=1, stride_axis=0)


def core_kernel(
    batch,
    recv_ref,
    fwd_hi,
    fwd_lo,
    rev_hi,
    rev_lo,
    mix_hi,
    mix_lo,
    band_hi,
    band_lo,
    flip_ref,
    prm_ref,
    out_ref,
    rows,
    g_re,
    g_im,
    d_re,
    d_im,
    z_re,
    z_im,
    v_re,
    v_im,
    x_re,
    x_im,
    base,
    outs,
):
    sources = recv_ref.shape[0] // ROWS_IN
    chunks = sources // batch
    poles = prm_ref.shape[1]
    span = poles
    half = poles // 2
    rows[: sources * ROWS_IN, :] = recv_ref[...].astype(F32)

    def part(index):
        return rows[pl.ds(index, sources, stride=ROWS_IN), :]

    u_f = jnp.concatenate([part(0), part(1)], axis=1)
    g_f = jnp.concatenate([part(2), part(3)], axis=1)
    u_b, g_b = u_f.astype(BF16), g_f.astype(BF16)
    prm = prm_ref[...]

    def line(index):
        return prm[index : index + 1, :]

    def total(value):
        return jnp.sum(value, axis=0, keepdims=True)

    mirrored = dot(flip_ref[...], u_b, FLIP).astype(BF16)
    cross = dot(mirrored, g_b, PLAIN)
    lead = dot(u_b, rev_hi[...], FLIP) + dot(u_b, rev_lo[...], FLIP)
    for index, ref in enumerate((v_re, v_im, x_re, x_im)):
        ref[:sources, :] = lead[:, index * poles : (index + 1) * poles]
    near_back = dot(g_b, band_hi[...], FLIP) + dot(g_b, band_lo[...], FLIP)
    near_back = near_back + jnp.concatenate([line(14), line(15)], axis=1) * g_f
    blocks = [cross[k * span : (k + 1) * span, k * span : (k + 1) * span] for k in range(2)]
    lag = jnp.concatenate([total(diagonals(value)) for value in blocks], axis=1)
    lag_hi, lag_lo = halves(jnp.broadcast_to(lag, (16, 2 * span)))
    stacked = jnp.concatenate([g_b, lag_hi, lag_lo], axis=0)
    moments = dot(stacked, fwd_hi[...], FLIP) + dot(stacked, fwd_lo[...], FLIP)
    near = moments[sources : sources + 1] + moments[sources + 16 : sources + 17]
    moments = moments[:sources]
    for index, ref in enumerate((g_re, g_im, d_re, d_im)):
        ref[:sources, :] = moments[:, index * poles : (index + 1) * poles]
    e_re, e_im = line(0), line(1)
    a, b, c, d, s_re, s_im, t_re, t_im = (jnp.zeros((batch, poles), F32) for _ in range(8))
    for chunk in reversed(range(chunks)):
        at = pl.ds(chunk * batch, batch)
        z_re[at, :] = a
        z_im[at, :] = b
        if chunk < chunks - 1:
            p, q, x, y = v_re[at, :], v_im[at, :], x_re[at, :], x_im[at, :]
            s_re, s_im = s_re + (p * a - q * b), s_im + (p * b + q * a)
            t_re = t_re + (x * a - y * b) + (p * c - q * d)
            t_im = t_im + (x * b + y * a) + (p * d + q * c)
        if chunk > 0:
            m = c + span * a
            n = d + span * b
            a, b = (e_re * a - e_im * b) + g_re[at, :], (e_re * b + e_im * a) + g_im[at, :]
            c, d = (e_re * m - e_im * n) + d_re[at, :], (e_re * n + e_im * m) + d_im[at, :]
    s_re, s_im, t_re, t_im = total(s_re), total(s_im), total(t_re), total(t_im)

    state = jnp.concatenate([z_re[:sources, :], z_im[:sources, :]], axis=1)
    state_hi, state_lo = halves(state)
    back = dot(state_hi, mix_hi[...], PLAIN) + dot(state_lo, mix_hi[...], PLAIN)
    back = back + dot(state_hi, mix_lo[...], PLAIN)
    back = back + near_back
    for chan in range(2):
        base[chan, :sources, :] = back[:, chan * span : (chan + 1) * span]

    s_re = s_re + near[:, :poles]
    s_im = s_im + near[:, poles : 2 * poles]
    t_re = t_re + near[:, 2 * poles : 3 * poles]
    t_im = t_im + near[:, 3 * poles :]

    s, t = (s_re, s_im), (t_re, t_im)
    ct, lift = (line(2), line(3)), (line(4), line(5))
    slope, curve = (line(6), line(7)), (line(8), line(9))
    size, pole_re, w = line(10), line(11), (line(12), line(13))
    by_c = times(s, lift)
    first, second = times(s, slope), times(t, ct)
    by_w = (first[0] + second[0], first[1] + second[1])
    third = times(s, curve)
    by_a = (size * second[0] + third[0], size * second[1] + third[1])
    by_dt = 2.0 * (by_w[0] * w[0] - by_w[1] * w[1])
    lane = lax.broadcasted_iota(jnp.int32, (1, poles), 1)
    by_skip = total(u_f * g_f)
    loose = [
        jnp.sum(jnp.where(lane < half, by_dt, 0.0), axis=1, keepdims=True),
        jnp.sum(jnp.where(lane < half, 0.0, by_dt), axis=1, keepdims=True),
        jnp.sum(by_skip[:, :span], axis=1, keepdims=True),
        jnp.sum(by_skip[:, span:], axis=1, keepdims=True),
    ]
    misc = jnp.zeros((1, poles), F32)
    for index, value in enumerate(loose):
        misc = jnp.where(lane == index, value, misc)
    lines = [
        2.0 * by_a[0] * pole_re,
        -2.0 * by_a[1],
        2.0 * by_c[0],
        -2.0 * by_c[1],
        misc,
        jnp.zeros((1, poles), F32),
    ]
    chips = sources // 2
    for core in range(2):
        for chan in range(2):
            outs[pl.ds(2 * core + chan, chips, stride=ROWS_OUT), :] = base[
                chan, pl.ds(core, chips, stride=2), :
            ]
    for index, value in enumerate(lines):
        outs[pl.ds(4 + index, chips, stride=ROWS_OUT), :] = jnp.broadcast_to(value, (chips, poles))
    out_ref[...] = outs[: chips * ROWS_OUT, :].astype(BF16)


def finish_kernel(core_ref, mine_ref, other_ref, grad_ref, a_ref, b_ref, c_ref, d_ref, dt_ref, skip_ref, rows):
    used = mine_ref.shape[0]
    chips = used // ROWS_OUT
    half = a_ref.shape[0]
    core = core_ref[0] & 1
    rows[0, :used, :] = mine_ref[...].astype(F32)
    rows[1, :used, :] = other_ref[...].astype(F32)
    odd = core ^ (core_ref[0] >> 1)

    def turned(owner, index):
        halves = [
            rows[odd ^ owner ^ pair, pl.ds(index + ROWS_OUT * pair, chips // 2, stride=2 * ROWS_OUT), :]
            for pair in range(2)
        ]
        return jnp.concatenate(halves, axis=0).T

    for owner in range(2):
        for chan in range(2):
            at = (2 * chan + owner) * chips
            grad_ref[:, at : at + chips] = turned(owner, 2 * core + chan).astype(BF16)
        for index, ref in enumerate((a_ref, b_ref, c_ref, d_ref)):
            block = turned(owner, 4 + index)
            for chan in range(2):
                at = (2 * chan + owner) * chips
                ref[:, at : at + chips] = block[chan * half : (chan + 1) * half]
        misc = turned(owner, 8)
        for chan in range(2):
            at = (2 * chan + owner) * chips
            dt_ref[:, at : at + chips] = misc[chan : chan + 1]
            skip_ref[:, at : at + chips] = misc[2 + chan : 3 + chan]


def lifted(w, growth, rise):
    tail = (jnp.full_like(w[0], SERIES[-1]), jnp.zeros_like(w[0]))
    for value in reversed(SERIES[:-1]):
        tail = times(tail, w)
        tail = (tail[0] + value, tail[1])
    near = times(times(w, w), tail)
    far = times(w, growth)
    small = w[0] * w[0] + w[1] * w[1] < 0.25
    return tuple(jnp.where(small, near[k], far[k] - rise[k]) for k in range(2))


def pole_lines(step_size, pole_re, a_im, c_re, c_im):
    w = (step_size * pole_re, step_size * a_im)
    growth = jnp.exp(w[0])
    cosine, sine = jnp.cos(w[1]), jnp.sin(w[1])
    half_sin = jnp.sin(0.5 * w[1])
    rise = (jnp.expm1(w[0]) * cosine - 2.0 * half_sin * half_sin, growth * sine)
    growth = (growth * cosine, growth * sine)
    modulus = pole_re * pole_re + a_im * a_im
    inverse = (pole_re / modulus, -a_im / modulus)
    c = (c_re, c_im)
    lift = times(rise, inverse)
    slope = times(times(growth, c), inverse)
    curve = times(times(times(lifted(w, growth, rise), inverse), inverse), c)
    return w + times(lift, c) + lift + slope + curve


def vmem(count):
    return [pl.BlockSpec(memory_space=pltpu.VMEM)] * count


def body(inputs, grad_out, log_dt, log_a_re, a_im, c_re, c_im, skip_gain):
    batch = lax.axis_size("dpair") * lax.axis_size("core")
    devices = batch * lax.axis_size("ctx")
    span, channels = inputs.shape[1:]
    poles = a_im.shape[1]
    assert channels == 2 * devices and span == 2 * poles
    chips = devices // 2
    place = lax.axis_index("core") * chips + lax.axis_index(("dpair", "ctx"))

    sent = pl.pallas_call(
        send_kernel,
        out_shape=jax.ShapeDtypeStruct((devices * ROWS_IN, span), BF16),
        in_specs=[pl.BlockSpec(memory_space=pltpu.HBM)] * 2,
        out_specs=pl.BlockSpec(memory_space=pltpu.HBM),
        scratch_shapes=[
            pltpu.VMEM((2, span, channels), BF16),
            pltpu.VMEM(((devices + 2 * SPARE) * ROWS_IN, span), F32),
            pltpu.VMEM((devices * ROWS_IN, span), BF16),
            pltpu.SemaphoreType.DMA((2 + SEND_PIECES,)),
        ],
    )(inputs[0], grad_out[0])
    recv = lax.all_to_all(
        sent.reshape(devices, ROWS_IN, span), OWNER, split_axis=0, concat_axis=0, tiled=True
    ).reshape(devices * ROWS_IN, span)

    def own(value):
        turned = value.T
        pair = [
            lax.dynamic_slice_in_dim(turned, place + k * devices, 1, axis=1) for k in range(2)
        ]
        return jnp.concatenate(pair, axis=0)[:, 0]

    def own_flat(value):
        pair = [lax.dynamic_slice_in_dim(value, place + k * devices, 1) for k in range(2)]
        return jnp.repeat(jnp.concatenate(pair), poles)

    step_size = jnp.exp(own_flat(log_dt))
    pole_re = -jnp.exp(own(log_a_re))
    im = own(a_im)
    terms = pole_lines(step_size, pole_re, im, own(c_re), own(c_im))
    w_re, w_im, ct_re, ct_im = terms[:4]
    far = jnp.exp(w_re * span)
    gains = [
        jnp.broadcast_to(lax.dynamic_slice_in_dim(skip_gain, place + k * devices, 1), (span,))
        for k in range(2)
    ]
    prm = jnp.stack(
        [far * jnp.cos(w_im * span), far * jnp.sin(w_im * span)]
        + list(terms[2:])
        + [step_size, pole_re, w_re, w_im]
        + gains
    )
    cols = jnp.stack([w_re, w_im, ct_re, ct_im], axis=1)
    wide = 2 * span
    tall = jax.ShapeDtypeStruct((4 * 2 * poles, wide), BF16)
    square = jax.ShapeDtypeStruct((wide, wide), BF16)
    tables = pl.pallas_call(
        table_kernel,
        out_shape=[tall] * 4 + [square] * 5,
        in_specs=vmem(1),
        out_specs=vmem(9),
        compiler_params=LIMIT,
    )(cols)
    grid = pltpu.VMEM((devices + SPARE, span), F32)
    answer = pl.pallas_call(
        functools.partial(core_kernel, batch),
        out_shape=jax.ShapeDtypeStruct((chips * ROWS_OUT, span), BF16),
        in_specs=vmem(11),
        out_specs=vmem(1)[0],
        scratch_shapes=[pltpu.VMEM(((devices + SPARE) * ROWS_IN, span), F32)]
        + [grid] * 10
        + [pltpu.VMEM((2, devices + 2 * SPARE, span), F32)]
        + [pltpu.VMEM(((chips + SPARE) * ROWS_OUT, span), F32)],
        compiler_params=LIMIT,
    )(recv, *tables, prm)
    groups = [[2 * chip + (first + chip) % 2 for chip in range(chips)] for first in range(2)]
    mine = lax.all_to_all(
        answer.reshape(chips, ROWS_OUT // 2, 2, span),
        OWNER,
        split_axis=0,
        concat_axis=0,
        tiled=True,
        axis_index_groups=groups,
    ).reshape(chips * ROWS_OUT, span)
    other = lax.ppermute(mine, "core", [(0, 1), (1, 0)])
    line = jax.ShapeDtypeStruct((poles, channels), F32)
    single = jax.ShapeDtypeStruct((1, channels), F32)
    results = pl.pallas_call(
        finish_kernel,
        out_shape=[jax.ShapeDtypeStruct((span, channels), BF16)] + [line] * 4 + [single] * 2,
        in_specs=[pl.BlockSpec(memory_space=pltpu.SMEM)] + vmem(2),
        out_specs=vmem(7),
        scratch_shapes=[pltpu.VMEM((2, (chips + SPARE) * ROWS_OUT, span), F32)],
        compiler_params=LIMIT,
    )((lax.axis_index("core") + 2 * lax.axis_index("dpair")).reshape(1), mine, other)
    return (
        results[0][None],
        results[5].reshape(channels),
        results[1].T,
        results[2].T,
        results[3].T,
        results[4].T,
        results[6].reshape(channels),
    )


def solution(mesh):
    pairs, ctx = mesh.devices.shape[0] // 2, mesh.devices.shape[1]
    fine = Mesh(mesh.devices.reshape(pairs, 2, ctx), ("dpair", "core", "ctx"))
    block = P(("dpair", "core"), "ctx", None)
    return jax.shard_map(
        body,
        mesh=fine,
        in_specs=(block, block, P(), P(), P(), P(), P(), P()),
        out_specs=(block, P(), P(), P(), P(), P(), P()),
        check_vma=False,
    )
```

```python
import functools
import math

import jax
import jax.numpy as jnp
from jax import lax
from jax.experimental import pallas as pl
from jax.experimental.pallas import tpu as pltpu
from jax.sharding import Mesh
from jax.sharding import PartitionSpec as P

OWNER = ("ctx", "dpair", "core")
F32 = jnp.float32
BF16 = jnp.bfloat16
ROWS_IN = 4
ROWS_OUT = 10
SEND_PIECES = 4
SPARE = 8
SERIES = [(k - 1) / math.factorial(k) for k in range(2, 12)]
LIMIT = pltpu.CompilerParams(vmem_limit_bytes=16 * 1024 * 1024)
FLIP = (((1,), (1,)), ((), ()))
PLAIN = (((1,), (0,)), ((), ()))
OUTER = (((0,), (0,)), ((), ()))


def halves(value):
    high = value.astype(BF16)
    low = (value - high.astype(F32)).astype(BF16)
    return (high, low)


def times(p, q):
    return (p[0] * q[0] - p[1] * q[1], p[0] * q[1] + p[1] * q[0])


def dot(a, b, dims):
    return lax.dot_general(a, b, dims, preferred_element_type=F32)


def send_kernel(inputs_ref, grad_ref, out_ref, stage, rows, packed, sems):
    owners = packed.shape[0] // ROWS_IN
    chips = owners // 2
    loads = [
        pltpu.make_async_copy(ref, stage.at[part], sems.at[part])
        for part, ref in enumerate((inputs_ref, grad_ref))
    ]
    for load in loads:
        load.start()
    for part, load in enumerate(loads):
        load.wait()
        for half in range(2):
            for core in range(2):
                at = half * owners + core * chips
                piece = stage[part, :, at : at + chips].astype(F32).T
                for pair in range(2):
                    line = ROWS_IN * (2 * pair + core) + 2 * part + half
                    rows[pl.ds(line, chips // 2, stride=4 * ROWS_IN), :] = piece[
                        pair * chips // 2 : (pair + 1) * chips // 2
                    ]
    pieces = sems.shape[0] - 2
    size = packed.shape[0] // pieces
    stores = []
    for index in range(pieces):
        at = pl.ds(index * size, size)
        packed[at, :] = rows[at, :].astype(BF16)
        stores.append(pltpu.make_async_copy(packed.at[at, :], out_ref.at[at, :], sems.at[2 + index]))
        stores[-1].start()
    for store in stores:
        store.wait()


def table_kernel(cols_ref, fwd_hi, fwd_lo, rev_hi, rev_lo, mix_hi, mix_lo, band_hi, band_lo, flip_ref):
    poles = cols_ref.shape[0]
    half = poles // 2
    span = poles
    w_re, w_im = cols_ref[:, 0:1], cols_ref[:, 1:2]
    ct_re, ct_im = cols_ref[:, 2:3], cols_ref[:, 3:4]
    lane = lax.broadcasted_iota(jnp.int32, (poles, span), 1)
    sub = lax.broadcasted_iota(jnp.int32, (poles, span), 0)
    first = sub < half

    def spread(value):
        return jnp.concatenate([jnp.where(first, value, 0.0), jnp.where(first, 0.0, value)], axis=1)

    def put(hi_ref, lo_ref, part, value):
        hi, lo = halves(spread(value))
        hi_ref[part * poles : (part + 1) * poles, :] = hi
        lo_ref[part * poles : (part + 1) * poles, :] = lo

    step = lane.astype(F32)
    grow = jnp.exp(w_re * step)
    turn = w_im * step
    f_re, f_im = grow * jnp.cos(turn), grow * jnp.sin(turn)
    put(fwd_hi, fwd_lo, 0, f_re)
    put(fwd_hi, fwd_lo, 1, f_im)
    put(fwd_hi, fwd_lo, 2, f_re * step)
    put(fwd_hi, fwd_lo, 3, f_im * step)
    back = (span - lane).astype(F32)
    shrink = jnp.exp(w_re * back)
    twist = w_im * back
    h_re, h_im = shrink * jnp.cos(twist), shrink * jnp.sin(twist)
    put(rev_hi, rev_lo, 0, h_re)
    put(rev_hi, rev_lo, 1, h_im)
    put(rev_hi, rev_lo, 2, h_re * back)
    put(rev_hi, rev_lo, 3, h_im * back)
    put(mix_hi, mix_lo, 0, 2.0 * (ct_re * h_re - ct_im * h_im))
    put(mix_hi, mix_lo, 1, -2.0 * (ct_re * h_im + ct_im * h_re))
    taps = 2.0 * (ct_re * f_re - ct_im * f_im)
    upper = lane >= sub
    zero = jnp.zeros((span, span), F32)
    for chan in range(2):
        line = jnp.sum(taps[chan * half : (chan + 1) * half, :], axis=0, keepdims=True)
        band = pltpu.roll(jnp.broadcast_to(line, (span, span)), 0, 1, stride=1, stride_axis=0)
        band = jnp.where(upper, band, 0.0)
        wide = jnp.concatenate([band, zero] if chan == 0 else [zero, band], axis=1)
        hi, lo = halves(wide)
        band_hi[chan * span : (chan + 1) * span, :] = hi
        band_lo[chan * span : (chan + 1) * span, :] = lo
    wide_sub = lax.broadcasted_iota(jnp.int32, flip_ref.shape, 0)
    wide_lane = lax.broadcasted_iota(jnp.int32, flip_ref.shape, 1)
    same = (wide_sub < span) == (wide_lane < span)
    mirror = (wide_sub % span) + (wide_lane % span) == span - 1
    flip_ref[...] = jnp.where(same & mirror, 1.0, 0.0).astype(BF16)


def diagonals(value):
    sub = lax.broadcasted_iota(jnp.int32, value.shape, 0)
    lane = lax.broadcasted_iota(jnp.int32, value.shape, 1)
    value = jnp.where(lane + sub >= value.shape[0] - 1, value, 0.0)
    return pltpu.roll(value, 1, 1, stride=1, stride_axis=0)


def core_kernel(
    batch,
    recv_ref,
    fwd_hi,
    fwd_lo,
    rev_hi,
    rev_lo,
    mix_hi,
    mix_lo,
    band_hi,
    band_lo,
    flip_ref,
    prm_ref,
    out_ref,
    rows,
    g_re,
    g_im,
    d_re,
    d_im,
    z_re,
    z_im,
    v_re,
    v_im,
    x_re,
    x_im,
    base,
    outs,
):
    sources = recv_ref.shape[0] // ROWS_IN
    chunks = sources // batch
    poles = prm_ref.shape[1]
    span = poles
    half = poles // 2
    rows[: sources * ROWS_IN, :] = recv_ref[...].astype(F32)

    def part(index):
        return rows[pl.ds(index, sources, stride=ROWS_IN), :]

    u_f = jnp.concatenate([part(0), part(1)], axis=1)
    g_f = jnp.concatenate([part(2), part(3)], axis=1)
    u_b, g_b = u_f.astype(BF16), g_f.astype(BF16)
    prm = prm_ref[...]

    def line(index):
        return prm[index : index + 1, :]

    def total(value):
        return jnp.sum(value, axis=0, keepdims=True)

    mirrored = dot(flip_ref[...], u_b, FLIP).astype(BF16)
    cross = dot(mirrored, g_b, PLAIN)
    lead = dot(u_b, rev_hi[...], FLIP) + dot(u_b, rev_lo[...], FLIP)
    for index, ref in enumerate((v_re, v_im, x_re, x_im)):
        ref[:sources, :] = lead[:, index * poles : (index + 1) * poles]
    near_back = dot(g_b, band_hi[...], FLIP) + dot(g_b, band_lo[...], FLIP)
    near_back = near_back + jnp.concatenate([line(14), line(15)], axis=1) * g_f
    blocks = [cross[k * span : (k + 1) * span, k * span : (k + 1) * span] for k in range(2)]
    lag = jnp.concatenate([total(diagonals(value)) for value in blocks], axis=1)
    lag_hi, lag_lo = halves(jnp.broadcast_to(lag, (16, 2 * span)))
    stacked = jnp.concatenate([g_b, lag_hi, lag_lo], axis=0)
    moments = dot(stacked, fwd_hi[...], FLIP) + dot(stacked, fwd_lo[...], FLIP)
    near = moments[sources : sources + 1] + moments[sources + 16 : sources + 17]
    moments = moments[:sources]
    for index, ref in enumerate((g_re, g_im, d_re, d_im)):
        ref[:sources, :] = moments[:, index * poles : (index + 1) * poles]
    e_re, e_im = line(0), line(1)
    a, b, c, d, s_re, s_im, t_re, t_im = (jnp.zeros((batch, poles), F32) for _ in range(8))
    for chunk in reversed(range(chunks)):
        at = pl.ds(chunk * batch, batch)
        z_re[at, :] = a
        z_im[at, :] = b
        if chunk < chunks - 1:
            p, q, x, y = v_re[at, :], v_im[at, :], x_re[at, :], x_im[at, :]
            s_re, s_im = s_re + (p * a - q * b), s_im + (p * b + q * a)
            t_re = t_re + (x * a - y * b) + (p * c - q * d)
            t_im = t_im + (x * b + y * a) + (p * d + q * c)
        if chunk > 0:
            m, n = e_re * a - e_im * b, e_re * b + e_im * a
            a, b = m + g_re[at, :], n + g_im[at, :]
            m, n = span * m + d_re[at, :], span * n + d_im[at, :]
            c, d = (e_re * c - e_im * d) + m, (e_re * d + e_im * c) + n
    s_re, s_im, t_re, t_im = total(s_re), total(s_im), total(t_re), total(t_im)

    state = jnp.concatenate([z_re[:sources, :], z_im[:sources, :]], axis=1)
    state_hi, state_lo = halves(state)
    back = dot(state_hi, mix_hi[...], PLAIN) + dot(state_lo, mix_hi[...], PLAIN)
    back = back + dot(state_hi, mix_lo[...], PLAIN)
    back = back + near_back
    for chan in range(2):
        base[chan, :sources, :] = back[:, chan * span : (chan + 1) * span]

    s_re = s_re + near[:, :poles]
    s_im = s_im + near[:, poles : 2 * poles]
    t_re = t_re + near[:, 2 * poles : 3 * poles]
    t_im = t_im + near[:, 3 * poles :]

    s, t = (s_re, s_im), (t_re, t_im)
    ct, lift = (line(2), line(3)), (line(4), line(5))
    slope, curve = (line(6), line(7)), (line(8), line(9))
    size, pole_re, w = line(10), line(11), (line(12), line(13))
    by_c = times(s, lift)
    first, second = times(s, slope), times(t, ct)
    by_w = (first[0] + second[0], first[1] + second[1])
    third = times(s, curve)
    by_a = (size * second[0] + third[0], size * second[1] + third[1])
    by_dt = 2.0 * (by_w[0] * w[0] - by_w[1] * w[1])
    lane = lax.broadcasted_iota(jnp.int32, (1, poles), 1)
    by_skip = total(u_f * g_f)
    loose = [
        jnp.sum(jnp.where(lane < half, by_dt, 0.0), axis=1, keepdims=True),
        jnp.sum(jnp.where(lane < half, 0.0, by_dt), axis=1, keepdims=True),
        jnp.sum(by_skip[:, :span], axis=1, keepdims=True),
        jnp.sum(by_skip[:, span:], axis=1, keepdims=True),
    ]
    misc = jnp.zeros((1, poles), F32)
    for index, value in enumerate(loose):
        misc = jnp.where(lane == index, value, misc)
    lines = [
        2.0 * by_a[0] * pole_re,
        -2.0 * by_a[1],
        2.0 * by_c[0],
        -2.0 * by_c[1],
        misc,
        jnp.zeros((1, poles), F32),
    ]
    chips = sources // 2
    for core in range(2):
        for chan in range(2):
            outs[pl.ds(2 * core + chan, chips, stride=ROWS_OUT), :] = base[
                chan, pl.ds(core, chips, stride=2), :
            ]
    for index, value in enumerate(lines):
        outs[pl.ds(4 + index, chips, stride=ROWS_OUT), :] = jnp.broadcast_to(value, (chips, poles))
    out_ref[...] = outs[: chips * ROWS_OUT, :].astype(BF16)


def finish_kernel(core_ref, mine_ref, other_ref, grad_ref, a_ref, b_ref, c_ref, d_ref, dt_ref, skip_ref, rows):
    used = mine_ref.shape[0]
    chips = used // ROWS_OUT
    half = a_ref.shape[0]
    core = core_ref[0] & 1
    rows[0, :used, :] = mine_ref[...].astype(F32)
    rows[1, :used, :] = other_ref[...].astype(F32)
    odd = core ^ (core_ref[0] >> 1)

    def turned(owner, index):
        halves = [
            rows[odd ^ owner ^ pair, pl.ds(index + ROWS_OUT * pair, chips // 2, stride=2 * ROWS_OUT), :]
            for pair in range(2)
        ]
        return jnp.concatenate(halves, axis=0).T

    for owner in range(2):
        for chan in range(2):
            at = (2 * chan + owner) * chips
            grad_ref[:, at : at + chips] = turned(owner, 2 * core + chan).astype(BF16)
        for index, ref in enumerate((a_ref, b_ref, c_ref, d_ref)):
            block = turned(owner, 4 + index)
            for chan in range(2):
                at = (2 * chan + owner) * chips
                ref[:, at : at + chips] = block[chan * half : (chan + 1) * half]
        misc = turned(owner, 8)
        for chan in range(2):
            at = (2 * chan + owner) * chips
            dt_ref[:, at : at + chips] = misc[chan : chan + 1]
            skip_ref[:, at : at + chips] = misc[2 + chan : 3 + chan]


def lifted(w, growth, rise):
    tail = (jnp.full_like(w[0], SERIES[-1]), jnp.zeros_like(w[0]))
    for value in reversed(SERIES[:-1]):
        tail = times(tail, w)
        tail = (tail[0] + value, tail[1])
    near = times(times(w, w), tail)
    far = times(w, growth)
    small = w[0] * w[0] + w[1] * w[1] < 0.25
    return tuple(jnp.where(small, near[k], far[k] - rise[k]) for k in range(2))


def pole_lines(step_size, pole_re, a_im, c_re, c_im):
    w = (step_size * pole_re, step_size * a_im)
    growth = jnp.exp(w[0])
    cosine, sine = jnp.cos(w[1]), jnp.sin(w[1])
    half_sin = jnp.sin(0.5 * w[1])
    rise = (jnp.expm1(w[0]) * cosine - 2.0 * half_sin * half_sin, growth * sine)
    growth = (growth * cosine, growth * sine)
    modulus = pole_re * pole_re + a_im * a_im
    inverse = (pole_re / modulus, -a_im / modulus)
    c = (c_re, c_im)
    lift = times(rise, inverse)
    slope = times(times(growth, c), inverse)
    curve = times(times(times(lifted(w, growth, rise), inverse), inverse), c)
    return w + times(lift, c) + lift + slope + curve


def vmem(count):
    return [pl.BlockSpec(memory_space=pltpu.VMEM)] * count


def body(inputs, grad_out, log_dt, log_a_re, a_im, c_re, c_im, skip_gain):
    batch = lax.axis_size("dpair") * lax.axis_size("core")
    devices = batch * lax.axis_size("ctx")
    span, channels = inputs.shape[1:]
    poles = a_im.shape[1]
    assert channels == 2 * devices and span == 2 * poles
    chips = devices // 2
    place = lax.axis_index("core") * chips + lax.axis_index(("dpair", "ctx"))

    sent = pl.pallas_call(
        send_kernel,
        out_shape=jax.ShapeDtypeStruct((devices * ROWS_IN, span), BF16),
        in_specs=[pl.BlockSpec(memory_space=pltpu.HBM)] * 2,
        out_specs=pl.BlockSpec(memory_space=pltpu.HBM),
        scratch_shapes=[
            pltpu.VMEM((2, span, channels), BF16),
            pltpu.VMEM(((devices + 2 * SPARE) * ROWS_IN, span), F32),
            pltpu.VMEM((devices * ROWS_IN, span), BF16),
            pltpu.SemaphoreType.DMA((2 + SEND_PIECES,)),
        ],
    )(inputs[0], grad_out[0])
    recv = lax.all_to_all(
        sent.reshape(devices, ROWS_IN, span), OWNER, split_axis=0, concat_axis=0, tiled=True
    ).reshape(devices * ROWS_IN, span)

    def own(value):
        turned = value.T
        pair = [
            lax.dynamic_slice_in_dim(turned, place + k * devices, 1, axis=1) for k in range(2)
        ]
        return jnp.concatenate(pair, axis=0)[:, 0]

    def own_flat(value):
        pair = [lax.dynamic_slice_in_dim(value, place + k * devices, 1) for k in range(2)]
        return jnp.repeat(jnp.concatenate(pair), poles)

    step_size = jnp.exp(own_flat(log_dt))
    pole_re = -jnp.exp(own(log_a_re))
    im = own(a_im)
    terms = pole_lines(step_size, pole_re, im, own(c_re), own(c_im))
    w_re, w_im, ct_re, ct_im = terms[:4]
    far = jnp.exp(w_re * span)
    gains = [
        jnp.broadcast_to(lax.dynamic_slice_in_dim(skip_gain, place + k * devices, 1), (span,))
        for k in range(2)
    ]
    prm = jnp.stack(
        [far * jnp.cos(w_im * span), far * jnp.sin(w_im * span)]
        + list(terms[2:])
        + [step_size, pole_re, w_re, w_im]
        + gains
    )
    cols = jnp.stack([w_re, w_im, ct_re, ct_im], axis=1)
    wide = 2 * span
    tall = jax.ShapeDtypeStruct((4 * 2 * poles, wide), BF16)
    square = jax.ShapeDtypeStruct((wide, wide), BF16)
    tables = pl.pallas_call(
        table_kernel,
        out_shape=[tall] * 4 + [square] * 5,
        in_specs=vmem(1),
        out_specs=vmem(9),
        compiler_params=LIMIT,
    )(cols)
    grid = pltpu.VMEM((devices + SPARE, span), F32)
    answer = pl.pallas_call(
        functools.partial(core_kernel, batch),
        out_shape=jax.ShapeDtypeStruct((chips * ROWS_OUT, span), BF16),
        in_specs=vmem(11),
        out_specs=vmem(1)[0],
        scratch_shapes=[pltpu.VMEM(((devices + SPARE) * ROWS_IN, span), F32)]
        + [grid] * 10
        + [pltpu.VMEM((2, devices + 2 * SPARE, span), F32)]
        + [pltpu.VMEM(((chips + SPARE) * ROWS_OUT, span), F32)],
        compiler_params=LIMIT,
    )(recv, *tables, prm)
    groups = [[2 * chip + (first + chip) % 2 for chip in range(chips)] for first in range(2)]
    mine = lax.all_to_all(
        answer.reshape(chips, ROWS_OUT // 2, 2, span),
        OWNER,
        split_axis=0,
        concat_axis=0,
        tiled=True,
        axis_index_groups=groups,
    ).reshape(chips * ROWS_OUT, span)
    other = lax.ppermute(mine, "core", [(0, 1), (1, 0)])
    line = jax.ShapeDtypeStruct((poles, channels), F32)
    single = jax.ShapeDtypeStruct((1, channels), F32)
    results = pl.pallas_call(
        finish_kernel,
        out_shape=[jax.ShapeDtypeStruct((span, channels), BF16)] + [line] * 4 + [single] * 2,
        in_specs=[pl.BlockSpec(memory_space=pltpu.SMEM)] + vmem(2),
        out_specs=vmem(7),
        scratch_shapes=[pltpu.VMEM((2, (chips + SPARE) * ROWS_OUT, span), F32)],
        compiler_params=LIMIT,
    )((lax.axis_index("core") + 2 * lax.axis_index("dpair")).reshape(1), mine, other)
    return (
        results[0][None],
        results[5].reshape(channels),
        results[1].T,
        results[2].T,
        results[3].T,
        results[4].T,
        results[6].reshape(channels),
    )


def solution(mesh):
    pairs, ctx = mesh.devices.shape[0] // 2, mesh.devices.shape[1]
    fine = Mesh(mesh.devices.reshape(pairs, 2, ctx), ("dpair", "core", "ctx"))
    block = P(("dpair", "core"), "ctx", None)
    return jax.shard_map(
        body,
        mesh=fine,
        in_specs=(block, block, P(), P(), P(), P(), P(), P()),
        out_specs=(block, P(), P(), P(), P(), P(), P()),
        check_vma=False,
    )
```
